768 devices in a mesh: dp: 64 (over x, y, core), mp: 12 (over z).
Axes of the slice: x: 4, y: 8, z: 12, core: 2. Of those that a mesh axis runs over, the one named last changes fastest.
Arguments:
- inputs: bfloat16 [128, 48, 4096], P('dp')
- denoiser: int32 [128], P('dp'), may hold values from 0 to 2
- span_mask: int32 [128, 48], P('dp'), may hold values 0 or 1
- lengths: int32 [128], P('dp'), may hold values from 12 to 48
- move_plan: int32 [128], P('dp'), may hold values from -1 to 1, as said below
- mode_table: bfloat16 [3, 4096], replicated, may hold values from -3 to 3
- sentinel: bfloat16 [4096], replicated, may hold values from -6 to 6
- w_query: bfloat16 [4096, 3072], P(None, 'mp')
- w_key: bfloat16 [4096, 3072], P(None, 'mp')
- w_value: bfloat16 [4096, 3072], P(None, 'mp'), may hold values from -0.09375 to 0.09375
- cotangent: bfloat16 [256, 48, 3072], P('dp', None, 'mp'), may hold values from -6 to 6
Outputs:
- context: bfloat16 [256, 48, 3072], P('dp', None, 'mp')
- input_grad: bfloat16 [128, 48, 4096], P('dp', 'mp')
The draws below stay inside these ranges and needn't reach their ends.
Inputs may be any that keep to these rules, and one draw needn't show every extreme that they name: `move_plan`: every row stays (0) or moves to the next (1) or previous (-1) data group along dp, cyclically. A data group sends at most one row to each of its two neighbours, and in every draw some data group receives a row from both neighbours.
All inputs are finite; a program needn't handle non-finite values. No bound on the sum of `span_mask` on one device may be relied on, other than what follows from the above.
Results may differ from the reference program's by a relative error of at most 0.02.
The reference program's roundings to bfloat16 on the way count: a program that leaves them out, or rounds other values in their place, can miss the bound.
Values may be sent and summed in bfloat16 or wider, within the bound.
No kernel may reach another device: no remote copies, remote signals or barrier semaphores. Data moves between devices by JAX's collectives and lax.ppermute only.
A program may use at most 64 MiB of HBM per device.

```python
import math
import jax
import jax.numpy as jnp
from jax import lax

D = 4096
HD = 256
HEADS = 12
LENGTH = 48
ROWS_DEV = 2
HOLD = 4
ROWS = 128
SLOTS = 256
MODES = 3
N_DP = 64


def draw_inputs(key, part):
    key = jax.random.fold_in(key, 3)
    keys = jax.random.split(key, 1)
    values = jax.random.normal(keys[0], (ROWS, LENGTH, D), jnp.float32)
    return values.astype(jnp.bfloat16)


def drawn_weight(key):
    values = jax.random.normal(key, (D, HEADS * HD), jnp.float32) / math.sqrt(D)
    return values.astype(jnp.bfloat16)


def draw_w_query(key, part):
    key = jax.random.fold_in(key, 5)
    return drawn_weight(key)


def draw_w_key(key, part):
    key = jax.random.fold_in(key, 7)
    return drawn_weight(key)


def draw_lengths(key, part):
    key = jax.random.fold_in(key, 11)
    keys = jax.random.split(key, 3)
    values = jax.random.randint(keys[0], (ROWS,), LENGTH // 4, LENGTH + 1)
    first = jax.random.randint(keys[1], (), 0, ROWS)
    second = (first + 1 + jax.random.randint(keys[2], (), 0, ROWS - 1)) % ROWS
    values = values.at[first].set(LENGTH)
    values = values.at[second].set(LENGTH // 4)
    return values.astype(jnp.int32)


def draw_move_plan(key, part):
    key = jax.random.fold_in(key, 13)
    keys = jax.random.split(key, 4)
    group_count = ROWS // ROWS_DEV
    scores = jax.random.randint(keys[0], (group_count, ROWS_DEV), 0, 2 ** 20) * ROWS_DEV
    scores = scores + jnp.arange(ROWS_DEV, dtype=jnp.int32)[None, :]
    order = jnp.argsort(scores, axis=1, stable=True).astype(jnp.int32)
    send_right = jax.random.randint(keys[1], (group_count,), 0, 2)
    send_left = jax.random.randint(keys[2], (group_count,), 0, 2)
    chosen = jax.random.randint(keys[3], (), 0, group_count)
    partner = (chosen + 2) % group_count
    groups = jnp.arange(group_count, dtype=jnp.int32)
    send_right = jnp.where(groups == chosen, 1, jnp.where(groups == partner, 0, send_right))
    send_left = jnp.where(groups == chosen, 0, jnp.where(groups == partner, 1, send_left))
    local = jnp.arange(ROWS_DEV, dtype=jnp.int32)[None, :]
    right_row = (local == order[:, 0:1]) & (send_right[:, None] == 1)
    left_row = (local == order[:, 1:2]) & (send_left[:, None] == 1)
    plan = jnp.where(right_row, 1, jnp.where(left_row, -1, 0))
    return plan.reshape(ROWS).astype(jnp.int32)


def with_ends(drawn, own_key, least, top_value):
    spot = [jax.random.randint(jax.random.fold_in(own_key, axis), (), 0, length) for axis, length in enumerate(drawn.shape)]
    main_axis = drawn.shape.index(max(drawn.shape))
    beside = spot[:main_axis] + [(spot[main_axis] + 1) % drawn.shape[main_axis]] + spot[main_axis + 1:]
    return drawn.at[tuple(spot)].set(least).at[tuple(beside)].set(top_value)


def block_scale(stream_key, extent, pieces, low, high):
    gain = 1.0
    for axis_at, shards_of in pieces:
        heights = jax.random.uniform(jax.random.fold_in(jax.random.fold_in(stream_key, 6), axis_at), (shards_of,), jnp.float32, low / len(pieces), high / len(pieces))
        gain = gain * jnp.repeat(jnp.exp(heights), extent[axis_at] // shards_of).reshape((-1,) + (1,) * (len(extent) - 1 - axis_at))
    return gain


def gaussian(rng, extent, spread, bound, cuts=(), kind=jnp.bfloat16):
    values = jax.random.normal(rng, extent, jnp.float32) * spread
    if len(cuts) > 0:
        values = block_scale(rng, extent, cuts, -0.22, 0.18) * values
    return jnp.clip(values, min=-bound, max=bound).astype(kind)


def setup_inputs(seed: int = 0) -> dict:
    key_list = jax.random.split(jax.random.key(seed), 12)
    return {
        "inputs": draw_inputs(jax.random.fold_in(key_list[11], 71), 0),
        "denoiser": with_ends(jax.random.randint(key_list[1], (ROWS,), 0, 3), jax.random.fold_in(key_list[1], 1), 0, 2).astype(jnp.int32),
        "span_mask": with_ends((jax.random.randint(key_list[2], (ROWS, LENGTH), 0, 20) < 3).astype(jnp.int32), jax.random.fold_in(key_list[2], 1), 0, 1),
        "lengths": draw_lengths(jax.random.fold_in(key_list[11], 71), 0),
        "move_plan": draw_move_plan(jax.random.fold_in(key_list[11], 71), 0),
        "mode_table": gaussian(key_list[5], (MODES, D), 0.5, 3.0),
        "sentinel": gaussian(key_list[6], (D,), 1.0, 6.0),
        "w_query": draw_w_query(jax.random.fold_in(key_list[11], 71), 0),
        "w_key": draw_w_key(jax.random.fold_in(key_list[11], 71), 0),
        "w_value": gaussian(key_list[9], (D, HEADS * HD), D ** -0.5, 0.09375, ((1, 12),)),
        "cotangent": gaussian(key_list[10], (SLOTS, LENGTH, HEADS * HD), 1.0, 6.0, ((0, 64), (2, 12))),
    }


def rounded(values):
    return lax.optimization_barrier(values.astype(jnp.bfloat16))

def attend_slot(slot_rows, slot_len, cotangent, w_query, w_key, w_value, query_full, key_full, value_full):
    flat_rows = slot_rows.astype(jnp.float32)
    inv_rms = lax.rsqrt(lax.optimization_barrier(jnp.mean(flat_rows * flat_rows, axis=1, keepdims=True)) + 1e-06)
    normed = flat_rows * inv_rms
    normed_b = normed.astype(jnp.bfloat16)

    def project(weight):
        result = jnp.dot(normed_b, weight, preferred_element_type=jnp.float32)
        return rounded(result).astype(jnp.float32).reshape(LENGTH, HEADS, HD)
    query_rows = project(w_query)
    key_rows = project(w_key)
    value_rows = project(w_value)
    positions = jnp.arange(LENGTH, dtype=jnp.int32)
    key_ok = (positions < jnp.maximum(slot_len, 1))[None, None, :]
    query_ok = positions < slot_len
    factor = 1.0 / math.sqrt(HD)
    scores = jnp.einsum('qhd,khd->hqk', query_rows, key_rows) * factor
    scores = jnp.where(key_ok, scores, -jnp.inf)
    row_max = lax.optimization_barrier(jnp.max(scores, axis=2, keepdims=True))
    exp_scores = jnp.exp(scores - row_max)
    soft = exp_scores / lax.optimization_barrier(jnp.sum(exp_scores, axis=2, keepdims=True))
    soft_b = rounded(soft).astype(jnp.float32)
    context = jnp.einsum('hqk,khd->qhd', soft_b, value_rows)
    context = context * query_ok[:, None, None].astype(jnp.float32)
    context = context.astype(jnp.bfloat16).reshape(LENGTH, HEADS * HD)
    grad_out = cotangent.reshape(LENGTH, HEADS, HD).astype(jnp.float32)
    grad_out = jnp.where(query_ok[:, None, None], grad_out, jnp.zeros_like(grad_out))
    grad_value = rounded(jnp.einsum('hqk,qhd->khd', soft_b, grad_out)).astype(jnp.float32)
    grad_soft = jnp.einsum('qhd,khd->hqk', grad_out, value_rows)
    row_inner = lax.optimization_barrier(jnp.sum(soft * grad_soft, axis=2, keepdims=True))
    grad_scores = rounded(soft * (grad_soft - row_inner) * factor).astype(jnp.float32)
    grad_query = rounded(jnp.einsum('hqk,khd->qhd', grad_scores, key_rows)).astype(jnp.float32)
    grad_key = rounded(jnp.einsum('hqk,qhd->khd', grad_scores, query_rows)).astype(jnp.float32)
    head_grad = jnp.einsum('qhd,ehd->hqe', grad_query, query_full)
    head_grad = head_grad + jnp.einsum('qhd,ehd->hqe', grad_key, key_full)
    head_grad = head_grad + jnp.einsum('qhd,ehd->hqe', grad_value, value_full)
    inner_norm = lax.optimization_barrier(jnp.mean(head_grad * normed[None, :, :], axis=2, keepdims=True))
    head_part = rounded((head_grad - normed[None, :, :] * inner_norm) * inv_rms[None, :, :])
    slot_grad = lax.optimization_barrier(jnp.sum(head_part.astype(jnp.float32), axis=0)).astype(jnp.bfloat16)
    return (context, slot_grad)

def reference(inputs, denoiser, span_mask, lengths, move_plan, mode_table, sentinel, w_query, w_key, w_value, cotangent):
    mode_rows = mode_table.astype(jnp.float32)[denoiser]
    span_flag = (span_mask == 1)[:, :, None]
    shaped = jnp.where(span_flag, sentinel.astype(jnp.float32)[None, None, :], inputs.astype(jnp.float32) + mode_rows[:, None, :]).astype(jnp.bfloat16)
    groups = jnp.arange(N_DP, dtype=jnp.int32)[:, None]
    local = jnp.arange(ROWS_DEV, dtype=jnp.int32)[None, :]
    moves = move_plan.reshape(N_DP, ROWS_DEV)
    target = jnp.where(moves == 1, (groups + 1) % N_DP * HOLD + ROWS_DEV, jnp.where(moves == -1, (groups + N_DP - 1) % N_DP * HOLD + ROWS_DEV + 1, groups * HOLD + local)).reshape(ROWS).astype(jnp.int32)
    sources = jnp.zeros((SLOTS,), jnp.int32).at[target].set(jnp.arange(ROWS, dtype=jnp.int32))
    filled = jnp.zeros((SLOTS,), jnp.bool_).at[target].set(True)
    slot_len = jnp.where(filled, lengths[sources], 0).astype(jnp.int32)
    query_full = w_query.astype(jnp.float32).reshape(D, HEADS, HD)
    key_full = w_key.astype(jnp.float32).reshape(D, HEADS, HD)
    value_full = w_value.astype(jnp.float32).reshape(D, HEADS, HD)

    def one_slot(slot):
        return attend_slot(shaped[sources[slot]], slot_len[slot], cotangent[slot], w_query, w_key, w_value, query_full, key_full, value_full)
    context, slot_grad = lax.map(one_slot, jnp.arange(SLOTS, dtype=jnp.int32))
    input_grad = slot_grad[target]
    input_grad = jnp.where(span_flag, jnp.zeros_like(input_grad), input_grad)
    return (context, input_grad)
```

```python
import math

import jax
import jax.numpy as jnp
from jax import lax
from jax.experimental import pallas as pl
from jax.experimental.pallas import tpu as pltpu
from jax.sharding import PartitionSpec as P

F32 = jnp.float32
BF16 = jnp.bfloat16
MIB = 1024 * 1024


def column(values):
    size = values.shape[1]
    diagonal = lax.broadcasted_iota(jnp.int32, (size, size), 0) == lax.broadcasted_iota(
        jnp.int32, (size, size), 1
    )
    spread = jnp.where(diagonal, jnp.broadcast_to(values, (size, size)).astype(F32), 0.0)
    return jnp.sum(spread, axis=1, keepdims=True)


def dot(a, b, contract):
    return lax.dot_general(a, b, (contract, ((), ())), preferred_element_type=F32)


def forward(
    chunk,
    inputs_hbm,
    w_query_hbm,
    w_key_hbm,
    w_value_hbm,
    span_ref,
    mode_ref,
    sentinel_ref,
    cotangent_ref,
    denoiser_ref,
    lengths_ref,
    move_ref,
    shaped_hbm,
    inv_ref,
    query_ref,
    key_ref,
    value_ref,
    soft_ref,
    context_ref,
    pay_mate_ref,
    pay_other_ref,
    inputs_v,
    shaped_v,
    w_v,
    in_sem,
    w_sem,
    out_sem,
):
    rows, length, width = inputs_v.shape
    tokens = rows * length
    head = w_v.shape[2]
    chunks = width // chunk
    weights = (w_query_hbm, w_key_hbm, w_value_hbm)

    load = pltpu.make_async_copy(inputs_hbm, inputs_v, in_sem)
    load.start()
    w_loads = []
    for c in range(chunks):
        part = []
        for i, weight in enumerate(weights):
            copy = pltpu.make_async_copy(
                weight.at[pl.ds(c * chunk, chunk)],
                w_v.at[i, pl.ds(c * chunk, chunk)],
                w_sem.at[i, c],
            )
            copy.start()
            part.append(copy)
        w_loads.append(part)

    span = [column(span_ref[r : r + 1, :]) == 1.0 for r in range(rows)]
    load.wait()
    squares = [jnp.zeros((length, 128), F32) for _ in range(rows)]
    for c in range(chunks):
        at = pl.ds(c * chunk, chunk)
        table = mode_ref[:, at].astype(F32)
        sentinel = sentinel_ref[:, at].astype(F32)
        for r in range(rows):
            kind = denoiser_ref[r]
            mode = jnp.where(kind == 0, table[0:1], jnp.where(kind == 1, table[1:2], table[2:3]))
            shaped = jnp.where(span[r], sentinel, inputs_v[r, :, at].astype(F32) + mode)
            shaped = shaped.astype(BF16)
            shaped_v[r * length : (r + 1) * length, at] = shaped
            wide = shaped.astype(F32)
            wide = wide * wide
            for k in range(0, chunk, 128):
                squares[r] = squares[r] + wide[:, k : k + 128]
    store = pltpu.make_async_copy(shaped_v, shaped_hbm, out_sem)
    store.start()
    mean = jnp.concatenate(squares, axis=0)
    mean = jnp.sum(mean, axis=1, keepdims=True) * (1.0 / width)
    inv_rms = lax.rsqrt(mean + 1e-06)
    inv_ref[...] = jnp.broadcast_to(inv_rms, inv_ref.shape)

    totals = [jnp.zeros((tokens, head), F32) for _ in weights]
    for c in range(chunks):
        at = pl.ds(c * chunk, chunk)
        normed = (shaped_v[:, at].astype(F32) * inv_rms).astype(BF16)
        for i in range(len(weights)):
            w_loads[c][i].wait()
            totals[i] = totals[i] + dot(normed, w_v[i, at, :], ((1,), (0,)))
    query, key, value = (total.astype(BF16) for total in totals)
    query_ref[...] = query
    key_ref[...] = key
    value_ref[...] = value

    factor = 1.0 / math.sqrt(head)
    q_at = lax.broadcasted_iota(jnp.int32, (tokens, tokens), 0)
    k_at = lax.broadcasted_iota(jnp.int32, (tokens, tokens), 1)
    ok = jnp.zeros((tokens, tokens), jnp.bool_)
    for r in range(rows):
        low = r * length
        high = low + jnp.maximum(lengths_ref[r], 1)
        ok = ok | (
            (q_at >= low) & (q_at < low + length) & (k_at >= low) & (k_at < high)
        )
    scores = jnp.where(ok, dot(query, key, ((1,), (1,))) * factor, -jnp.inf)
    exp_scores = jnp.exp(scores - jnp.max(scores, axis=1, keepdims=True))
    soft = exp_scores / jnp.sum(exp_scores, axis=1, keepdims=True)
    soft_ref[...] = soft
    context = dot(soft.astype(BF16), value, ((1,), (0,)))
    t_at = lax.broadcasted_iota(jnp.int32, (length, 1), 0)
    mine = []
    for r in range(rows):
        valid = t_at < lengths_ref[r]
        mine.append(jnp.where(valid, context[r * length : (r + 1) * length], 0.0))
    for r in range(rows):
        context_ref[r] = jnp.where(move_ref[r] == 0, mine[r], 0.0).astype(BF16)

    even = lax.rem(lax.axis_index("dp"), 2) == 0
    right = jnp.where(move_ref[0] == 1, mine[0], jnp.where(move_ref[1] == 1, mine[1], 0.0))
    left = jnp.where(move_ref[0] == -1, mine[0], jnp.where(move_ref[1] == -1, mine[1], 0.0))
    right = right.astype(BF16)
    left = left.astype(BF16)

    def pay(ref, to_right):
        ref[0:length, :] = jnp.where(to_right, right, left)
        ref[length : 2 * length, :] = jnp.where(
            to_right, cotangent_ref[rows + 1], cotangent_ref[rows]
        )

    pay(pay_mate_ref, even)
    pay(pay_other_ref, jnp.logical_not(even))
    store.wait()


def backward(
    chunk,
    w_query_hbm,
    w_key_hbm,
    w_value_hbm,
    shaped_hbm,
    inv_ref,
    query_ref,
    key_ref,
    value_ref,
    soft_ref,
    context_ref,
    cotangent_ref,
    got_mate_ref,
    got_other_ref,
    span_ref,
    lengths_ref,
    move_ref,
    out_ref,
    context_out_ref,
    shaped_v,
    w_v,
    grad_v,
    in_sem,
    w_sem,
):
    rows, length, head = context_ref.shape
    tokens, width = shaped_v.shape
    chunks = width // chunk
    weights = (w_query_hbm, w_key_hbm, w_value_hbm)

    w_loads = []
    for c in range(chunks):
        part = []
        for i, weight in enumerate(weights):
            copy = pltpu.make_async_copy(
                weight.at[pl.ds(c * chunk, chunk)],
                w_v.at[i, pl.ds(c * chunk, chunk)],
                w_sem.at[i, c],
            )
            copy.start()
            part.append(copy)
        w_loads.append(part)
        if c == 0:
            load = pltpu.make_async_copy(shaped_hbm, shaped_v, in_sem)
            load.start()

    even = lax.rem(lax.axis_index("dp"), 2) == 0
    got_mate = got_mate_ref[...]
    got_other = got_other_ref[...]
    from_right = jnp.where(even, got_mate, got_other)
    from_left = jnp.where(even, got_other, got_mate)
    for r in range(rows):
        context_out_ref[r] = context_ref[r]
    context_out_ref[rows] = from_left[0:length]
    context_out_ref[rows + 1] = from_right[0:length]

    t_at = lax.broadcasted_iota(jnp.int32, (length, 1), 0)
    grads = []
    for r in range(rows):
        move = move_ref[r]
        grad = jnp.where(
            move == 0,
            cotangent_ref[r],
            jnp.where(move == 1, from_right[length:], from_left[length:]),
        )
        grads.append(jnp.where(t_at < lengths_ref[r], grad.astype(F32), 0.0))
    grad_out = jnp.concatenate(grads, axis=0).astype(BF16)

    factor = 1.0 / math.sqrt(head)
    soft = soft_ref[...]
    grad_value = dot(soft.astype(BF16), grad_out, ((0,), (0,))).astype(BF16)
    grad_soft = dot(grad_out, value_ref[...], ((1,), (1,)))
    row_inner = jnp.sum(soft * grad_soft, axis=1, keepdims=True)
    grad_scores = (soft * (grad_soft - row_inner) * factor).astype(BF16)
    grad_query = dot(grad_scores, key_ref[...], ((1,), (0,))).astype(BF16)
    grad_key = dot(grad_scores, query_ref[...], ((0,), (0,))).astype(BF16)
    gradients = (grad_query, grad_key, grad_value)

    inv_rms = inv_ref[:, 0:1]
    load.wait()
    inner = jnp.zeros((tokens, 128), F32)
    for c in range(chunks):
        at = pl.ds(c * chunk, chunk)
        total = None
        for i in range(len(weights)):
            w_loads[c][i].wait()
            part = dot(gradients[i], w_v[i, at, :], ((1,), (1,)))
            total = part if total is None else total + part
        grad_v[:, at] = total
        product = total * (shaped_v[:, at].astype(F32) * inv_rms)
        for k in range(0, chunk, 128):
            inner = inner + product[:, k : k + 128]
    inner = jnp.sum(inner, axis=1, keepdims=True) * (1.0 / width)

    span = jnp.concatenate([column(span_ref[r : r + 1, :]) for r in range(rows)], axis=0)
    keep = span != 1.0
    pieces, per_row = out_ref.shape[0], out_ref.shape[1] // rows
    for c in range(chunks):
        at = pl.ds(c * chunk, chunk)
        normed = shaped_v[:, at].astype(F32) * inv_rms
        part = (grad_v[:, at] - normed * inner) * inv_rms
        part = jnp.where(keep, part, 0.0)
        for d in range(pieces):
            piece = [
                part[r * length + d * per_row : r * length + (d + 1) * per_row] for r in range(rows)
            ]
            out_ref[d, :, at] = jnp.concatenate(piece, axis=0).astype(BF16)


def exchange(array, pairs):
    return lax.ppermute(array, "dp", pairs)


def shards(
    inputs,
    denoiser,
    span_mask,
    lengths,
    move_plan,
    mode_table,
    sentinel,
    w_query,
    w_key,
    w_value,
    cotangent,
):
    rows, length, width = inputs.shape
    head = w_query.shape[1]
    tokens = rows * length
    groups = lax.axis_size("dp")
    members = lax.axis_size("mp")
    seg = length // members
    chunk = 512
    vmem = pl.BlockSpec(memory_space=pltpu.VMEM)
    smem = pl.BlockSpec(memory_space=pltpu.SMEM)
    hbm = pl.BlockSpec(memory_space=pl.ANY)

    def shape(dims, dtype):
        return jax.ShapeDtypeStruct(dims, dtype)

    shaped, inv_rms, query, key, value, soft, context, pay_mate, pay_other = pl.pallas_call(
        lambda *refs: forward(chunk, *refs),
        out_shape=(
            shape((tokens, width), BF16),
            shape((tokens, 128), F32),
            shape((tokens, head), BF16),
            shape((tokens, head), BF16),
            shape((tokens, head), BF16),
            shape((tokens, tokens), F32),
            shape((rows, length, head), BF16),
            shape((2 * length, head), BF16),
            shape((2 * length, head), BF16),
        ),
        in_specs=[hbm] * 4 + [vmem] * 4 + [smem] * 3,
        out_specs=[hbm] + [vmem] * 8,
        scratch_shapes=[
            pltpu.VMEM((rows, length, width), BF16),
            pltpu.VMEM((tokens, width), BF16),
            pltpu.VMEM((3, width, head), BF16),
            pltpu.SemaphoreType.DMA,
            pltpu.SemaphoreType.DMA((3, width // chunk)),
            pltpu.SemaphoreType.DMA,
        ],
        compiler_params=pltpu.CompilerParams(vmem_limit_bytes=40 * MIB),
        name="forward",
    )(
        inputs,
        w_query,
        w_key,
        w_value,
        span_mask,
        mode_table,
        sentinel.reshape(1, width),
        cotangent,
        denoiser,
        lengths,
        move_plan,
    )

    others = [(g, (g + 1) % groups if g % 2 else (g - 1) % groups) for g in range(groups)]
    got_other = exchange(pay_other, others)
    got_mate = exchange(pay_mate, [(g, g ^ 1) for g in range(groups)])

    head_part, context = pl.pallas_call(
        lambda *refs: backward(chunk, *refs),
        out_shape=(
            shape((members, rows * seg, width), BF16),
            shape((2 * rows, length, head), BF16),
        ),
        in_specs=[hbm] * 4 + [vmem] * 10 + [smem] * 2,
        out_specs=[vmem, vmem],
        scratch_shapes=[
            pltpu.VMEM((tokens, width), BF16),
            pltpu.VMEM((3, width, head), BF16),
            pltpu.VMEM((tokens, width), F32),
            pltpu.SemaphoreType.DMA,
            pltpu.SemaphoreType.DMA((3, width // chunk)),
        ],
        compiler_params=pltpu.CompilerParams(vmem_limit_bytes=40 * MIB),
        name="backward",
    )(
        w_query,
        w_key,
        w_value,
        shaped,
        inv_rms,
        query,
        key,
        value,
        soft,
        context,
        cotangent,
        got_mate,
        got_other,
        span_mask,
        lengths,
        move_plan,
    )
    summed = lax.psum_scatter(head_part, "mp", scatter_dimension=0)
    return (context, summed.reshape(rows, seg, width))


def solution(mesh):
    return jax.shard_map(
        shards,
        mesh=mesh,
        in_specs=(
            P("dp", None, None),
            P("dp"),
            P("dp", None),
            P("dp"),
            P("dp"),
            P(),
            P(),
            P(None, "mp"),
            P(None, "mp"),
            P(None, "mp"),
            P("dp", None, "mp"),
        ),
        out_specs=(P("dp", None, "mp"), P("dp", "mp", None)),
        check_vma=False,
    )
```

```python
import math

import jax
import jax.numpy as jnp
from jax import lax
from jax.experimental import pallas as pl
from jax.experimental.pallas import tpu as pltpu
from jax.sharding import PartitionSpec as P

F32 = jnp.float32
BF16 = jnp.bfloat16
MIB = 1024 * 1024


def column(values):
    size = values.shape[1]
    diagonal = lax.broadcasted_iota(jnp.int32, (size, size), 0) == lax.broadcasted_iota(
        jnp.int32, (size, size), 1
    )
    spread = jnp.where(diagonal, jnp.broadcast_to(values, (size, size)).astype(F32), 0.0)
    return jnp.sum(spread, axis=1, keepdims=True)


def dot(a, b, contract):
    return lax.dot_general(a, b, (contract, ((), ())), preferred_element_type=F32)


def forward(
    chunk,
    inputs_hbm,
    denoiser_hbm,
    span_hbm,
    lengths_hbm,
    move_hbm,
    mode_hbm,
    sentinel_hbm,
    w_query_hbm,
    w_key_hbm,
    w_value_hbm,
    cotangent_hbm,
    shaped_ref,
    w_ref,
    marks_ref,
    query_ref,
    key_ref,
    value_ref,
    soft_ref,
    context_ref,
    own_ref,
    pay_mate_ref,
    pay_other_ref,
    inputs_v,
    span_v,
    mode_v,
    sentinel_v,
    cotangent_v,
    denoiser_s,
    lengths_s,
    move_s,
    sem,
    w_sem,
):
    rows, length, width = inputs_v.shape
    tokens = rows * length
    head = w_ref.shape[2]
    chunks = width // chunk
    weights = (w_query_hbm, w_key_hbm, w_value_hbm)

    small = [
        pltpu.make_async_copy(source, target, sem.at[i])
        for i, (source, target) in enumerate(
            (
                (denoiser_hbm, denoiser_s),
                (span_hbm, span_v),
                (mode_hbm, mode_v),
                (sentinel_hbm, sentinel_v),
                (inputs_hbm, inputs_v),
                (lengths_hbm, lengths_s),
                (move_hbm, move_s),
                (cotangent_hbm, cotangent_v),
            )
        )
    ]
    for copy in small[:5]:
        copy.start()
    w_loads = []
    for c in range(chunks):
        part = []
        for i, weight in enumerate(weights):
            copy = pltpu.make_async_copy(
                weight.at[pl.ds(c * chunk, chunk)],
                w_ref.at[i, pl.ds(c * chunk, chunk)],
                w_sem.at[i, c],
            )
            copy.start()
            part.append(copy)
        w_loads.append(part)
    for copy in small[5:]:
        copy.start()

    for copy in small[:5]:
        copy.wait()
    span = [column(span_v[r : r + 1, :]) == 1.0 for r in range(rows)]
    squares = [jnp.zeros((length, 128), F32) for _ in range(rows)]
    for c in range(chunks):
        at = pl.ds(c * chunk, chunk)
        table = mode_v[:, at].astype(F32)
        sentinel = sentinel_v[at].astype(F32).reshape(1, chunk)
        for r in range(rows):
            kind = denoiser_s[r]
            mode = jnp.where(kind == 0, table[0:1], jnp.where(kind == 1, table[1:2], table[2:3]))
            shaped = jnp.where(span[r], sentinel, inputs_v[r, :, at].astype(F32) + mode)
            shaped = shaped.astype(BF16)
            shaped_ref[r * length : (r + 1) * length, at] = shaped
            wide = shaped.astype(F32)
            wide = wide * wide
            for k in range(0, chunk, 128):
                squares[r] = squares[r] + wide[:, k : k + 128]
    mean = jnp.concatenate(squares, axis=0)
    mean = jnp.sum(mean, axis=1, keepdims=True) * (1.0 / width)
    inv_rms = lax.rsqrt(mean + 1e-06)

    totals = [jnp.zeros((tokens, head), F32) for _ in weights]
    for c in range(chunks):
        at = pl.ds(c * chunk, chunk)
        normed = (shaped_ref[:, at].astype(F32) * inv_rms).astype(BF16)
        for i in range(len(weights)):
            w_loads[c][i].wait()
            totals[i] = totals[i] + dot(normed, w_ref[i, at, :], ((1,), (0,)))
    query, key, value = (total.astype(BF16) for total in totals)
    query_ref[...] = query
    key_ref[...] = key
    value_ref[...] = value

    for copy in small[5:]:
        copy.wait()
    factor = 1.0 / math.sqrt(head)
    q_at = lax.broadcasted_iota(jnp.int32, (tokens, tokens), 0)
    k_at = lax.broadcasted_iota(jnp.int32, (tokens, tokens), 1)
    ok = jnp.zeros((tokens, tokens), jnp.bool_)
    for r in range(rows):
        low = r * length
        high = low + jnp.maximum(lengths_s[r], 1)
        ok = ok | ((q_at >= low) & (q_at < low + length) & (k_at >= low) & (k_at < high))
    scores = jnp.where(ok, dot(query, key, ((1,), (1,))) * factor, -jnp.inf)
    exp_scores = jnp.exp(scores - jnp.max(scores, axis=1, keepdims=True))
    soft = exp_scores / jnp.sum(exp_scores, axis=1, keepdims=True)
    soft_ref[...] = soft
    context = dot(soft.astype(BF16), value, ((1,), (0,)))

    t_at = lax.broadcasted_iota(jnp.int32, (length, 128), 0)
    lane = lax.broadcasted_iota(jnp.int32, (length, 128), 1)
    mine = []
    for r in range(rows):
        move = move_s[r]
        valid = t_at < lengths_s[r]
        here = slice(r * length, (r + 1) * length)
        mine.append(jnp.where(valid[:, 0:1], context[here], 0.0))
        own = jnp.where(valid[:, 0:1], cotangent_v[r].astype(F32), 0.0)
        own_ref[here, :] = jnp.where(move == 0, own, 0.0).astype(BF16)
        context_ref[r] = jnp.where(move == 0, mine[r], 0.0).astype(BF16)
        marks = jnp.where(lane == 0, inv_rms[here], 0.0)
        marks = jnp.where((lane == 1) & valid & (move == 1), 1.0, marks)
        marks = jnp.where((lane == 2) & valid & (move == -1), 1.0, marks)
        marks_ref[here, :] = jnp.where((lane == 3) & jnp.logical_not(span[r]), 1.0, marks)

    even = lax.rem(lax.axis_index("dp"), 2) == 0
    right = jnp.where(move_s[0] == 1, mine[0], jnp.where(move_s[1] == 1, mine[1], 0.0))
    left = jnp.where(move_s[0] == -1, mine[0], jnp.where(move_s[1] == -1, mine[1], 0.0))
    right = right.astype(BF16)
    left = left.astype(BF16)

    def pay(ref, to_right):
        ref[0:length, :] = jnp.where(to_right, right, left)
        ref[length : 2 * length, :] = jnp.where(
            to_right, cotangent_v[rows + 1], cotangent_v[rows]
        )

    pay(pay_mate_ref, even)
    pay(pay_other_ref, jnp.logical_not(even))


def backward(
    chunk,
    shaped_ref,
    w_ref,
    marks_ref,
    query_ref,
    key_ref,
    value_ref,
    soft_ref,
    context_ref,
    own_ref,
    got_mate_ref,
    got_other_ref,
    out_ref,
    context_out_ref,
    grad_v,
):
    rows, length, head = context_ref.shape
    tokens, width = shaped_ref.shape
    chunks = width // chunk

    even = lax.rem(lax.axis_index("dp"), 2) == 0
    got_mate = got_mate_ref[...]
    got_other = got_other_ref[...]
    from_right = jnp.where(even, got_mate, got_other)
    from_left = jnp.where(even, got_other, got_mate)
    for r in range(rows):
        context_out_ref[r] = context_ref[r]
    context_out_ref[rows] = from_left[0:length]
    context_out_ref[rows + 1] = from_right[0:length]

    marks = marks_ref[...]
    inv_rms = marks[:, 0:1]
    right_grad = from_right[length:].astype(F32)
    left_grad = from_left[length:].astype(F32)
    right_grad = jnp.concatenate([right_grad] * rows, axis=0)
    left_grad = jnp.concatenate([left_grad] * rows, axis=0)
    grad_out = jnp.where(
        marks[:, 1:2] == 1.0,
        right_grad,
        jnp.where(marks[:, 2:3] == 1.0, left_grad, own_ref[...].astype(F32)),
    ).astype(BF16)

    factor = 1.0 / math.sqrt(head)
    soft = soft_ref[...]
    grad_value = dot(soft.astype(BF16), grad_out, ((0,), (0,))).astype(BF16)
    grad_soft = dot(grad_out, value_ref[...], ((1,), (1,)))
    row_inner = jnp.sum(soft * grad_soft, axis=1, keepdims=True)
    grad_scores = (soft * (grad_soft - row_inner) * factor).astype(BF16)
    grad_query = dot(grad_scores, key_ref[...], ((1,), (0,))).astype(BF16)
    grad_key = dot(grad_scores, query_ref[...], ((0,), (0,))).astype(BF16)
    gradients = (grad_query, grad_key, grad_value)

    inner = jnp.zeros((tokens, 128), F32)
    for c in range(chunks):
        at = pl.ds(c * chunk, chunk)
        total = None
        for i in range(3):
            part = dot(gradients[i], w_ref[i, at, :], ((1,), (1,)))
            total = part if total is None else total + part
        grad_v[:, at] = total
        product = total * (shaped_ref[:, at].astype(F32) * inv_rms)
        for k in range(0, chunk, 128):
            inner = inner + product[:, k : k + 128]
    inner = jnp.sum(inner, axis=1, keepdims=True) * (1.0 / width)

    keep = marks[:, 3:4] == 1.0
    pieces, _, per_row, _ = out_ref.shape
    for c in range(chunks):
        at = pl.ds(c * chunk, chunk)
        normed = shaped_ref[:, at].astype(F32) * inv_rms
        part = (grad_v[:, at] - normed * inner) * inv_rms
        part = jnp.where(keep, part, 0.0).astype(BF16)
        for d in range(pieces):
            for r in range(rows):
                first = r * length + d * per_row
                out_ref[d, r, :, at] = part[first : first + per_row]


def exchange(array, pairs):
    return lax.ppermute(array, "dp", pairs)


def shards(
    inputs,
    denoiser,
    span_mask,
    lengths,
    move_plan,
    mode_table,
    sentinel,
    w_query,
    w_key,
    w_value,
    cotangent,
):
    rows, length, width = inputs.shape
    head = w_query.shape[1]
    tokens = rows * length
    groups = lax.axis_size("dp")
    members = lax.axis_size("mp")
    seg = length // members
    chunk = 512
    vmem = pl.BlockSpec(memory_space=pltpu.VMEM)
    hbm = pl.BlockSpec(memory_space=pltpu.HBM)

    def shape(dims, dtype):
        return jax.ShapeDtypeStruct(dims, dtype)

    *kept, pay_mate, pay_other = pl.pallas_call(
        lambda *refs: forward(chunk, *refs),
        out_shape=(
            shape((tokens, width), BF16),
            shape((3, width, head), BF16),
            shape((tokens, 128), F32),
            shape((tokens, head), BF16),
            shape((tokens, head), BF16),
            shape((tokens, head), BF16),
            shape((tokens, tokens), F32),
            shape((rows, length, head), BF16),
            shape((tokens, head), BF16),
            shape((2 * length, head), BF16),
            shape((2 * length, head), BF16),
        ),
        in_specs=[hbm] * 11,
        out_specs=[vmem] * 11,
        scratch_shapes=[
            pltpu.VMEM((rows, length, width), BF16),
            pltpu.VMEM(span_mask.shape, jnp.int32),
            pltpu.VMEM(mode_table.shape, BF16),
            pltpu.VMEM((width,), BF16),
            pltpu.VMEM(cotangent.shape, BF16),
            pltpu.SMEM((rows,), jnp.int32),
            pltpu.SMEM((rows,), jnp.int32),
            pltpu.SMEM((rows,), jnp.int32),
            pltpu.SemaphoreType.DMA((8,)),
            pltpu.SemaphoreType.DMA((3, width // chunk)),
        ],
        compiler_params=pltpu.CompilerParams(vmem_limit_bytes=24 * MIB),
        name="forward",
    )(
        *(
            pltpu.with_memory_space_constraint(array, pltpu.HBM)
            for array in (
                inputs,
                denoiser,
                span_mask,
                lengths,
                move_plan,
                mode_table,
                sentinel,
                w_query,
                w_key,
                w_value,
                cotangent,
            )
        )
    )

    others = [(g, (g + 1) % groups if g % 2 else (g - 1) % groups) for g in range(groups)]
    got_other = exchange(pay_other, others)
    got_mate = exchange(pay_mate, [(g, g ^ 1) for g in range(groups)])

    head_part, context = pl.pallas_call(
        lambda *refs: backward(chunk, *refs),
        out_shape=(
            shape((members, rows, seg, width), BF16),
            shape((2 * rows, length, head), BF16),
        ),
        in_specs=[vmem] * 11,
        out_specs=[vmem, vmem],
        scratch_shapes=[pltpu.VMEM((tokens, width), F32)],
        compiler_params=pltpu.CompilerParams(vmem_limit_bytes=24 * MIB),
        name="backward",
    )(*kept, got_mate, got_other)
    heads = lax.all_to_all(head_part, "mp", 0, 0)
    return (context, jnp.sum(heads.astype(F32), axis=0).astype(BF16))


def solution(mesh):
    return jax.shard_map(
        shards,
        mesh=mesh,
        in_specs=(
            P("dp", None, None),
            P("dp"),
            P("dp", None),
            P("dp"),
            P("dp"),
            P(),
            P(),
            P(None, "mp"),
            P(None, "mp"),
            P(None, "mp"),
            P("dp", None, "mp"),
        ),
        out_specs=(P("dp", None, "mp"), P("dp", "mp", None)),
        check_vma=False,
    )
```

```python
import math

import jax
import jax.numpy as jnp
from jax import lax
from jax.experimental import pallas as pl
from jax.experimental.pallas import tpu as pltpu
from jax.sharding import PartitionSpec as P

F32 = jnp.float32
BF16 = jnp.bfloat16
MIB = 1024 * 1024


def column(values):
    size = values.shape[1]
    diagonal = lax.broadcasted_iota(jnp.int32, (size, size), 0) == lax.broadcasted_iota(
        jnp.int32, (size, size), 1
    )
    spread = jnp.where(diagonal, jnp.broadcast_to(values, (size, size)).astype(F32), 0.0)
    return jnp.sum(spread, axis=1, keepdims=True)


def dot(a, b, contract):
    return lax.dot_general(a, b, (contract, ((), ())), preferred_element_type=F32)


def is_even():
    return lax.rem(lax.axis_index("dp"), 2) == 0


def prepare(
    chunk,
    inputs_hbm,
    denoiser_hbm,
    span_hbm,
    lengths_hbm,
    move_hbm,
    mode_hbm,
    sentinel_hbm,
    cotangent_hbm,
    w_query_hbm,
    w_key_hbm,
    w_value_hbm,
    shaped_ref,
    normed_ref,
    w_ref,
    marks_ref,
    own_ref,
    pay_mate_ref,
    pay_other_ref,
    inputs_v,
    span_v,
    mode_v,
    sentinel_v,
    cotangent_v,
    denoiser_s,
    lengths_s,
    move_s,
    sem,
):
    rows, length, width = inputs_v.shape
    tokens = rows * length
    chunks = width // chunk
    copies = [
        pltpu.make_async_copy(source, target, sem.at[i])
        for i, (source, target) in enumerate(
            (
                (inputs_hbm, inputs_v),
                (cotangent_hbm, cotangent_v),
                (mode_hbm, mode_v),
                (sentinel_hbm, sentinel_v),
                (span_hbm, span_v),
                (denoiser_hbm, denoiser_s),
                (lengths_hbm, lengths_s),
                (move_hbm, move_s),
                (w_query_hbm, w_ref.at[0]),
                (w_key_hbm, w_ref.at[1]),
                (w_value_hbm, w_ref.at[2]),
            )
        )
    ]
    for copy in copies:
        copy.start()
    for copy in copies[:8]:
        copy.wait()

    even = is_even()
    to_right, to_left = cotangent_v[rows + 1], cotangent_v[rows]
    pay_mate_ref[...] = jnp.where(even, to_right, to_left)
    pay_other_ref[...] = jnp.where(even, to_left, to_right)

    span = [column(span_v[r : r + 1, :]) == 1.0 for r in range(rows)]
    squares = [jnp.zeros((length, 128), F32) for _ in range(rows)]
    for c in range(chunks):
        at = pl.ds(c * chunk, chunk)
        table = mode_v[:, at].astype(F32)
        sentinel = sentinel_v[at].astype(F32).reshape(1, chunk)
        for r in range(rows):
            kind = denoiser_s[r]
            mode = jnp.where(kind == 0, table[0:1], jnp.where(kind == 1, table[1:2], table[2:3]))
            shaped = jnp.where(span[r], sentinel, inputs_v[r, :, at].astype(F32) + mode)
            shaped = shaped.astype(BF16)
            shaped_ref[r * length : (r + 1) * length, at] = shaped
            wide = shaped.astype(F32)
            wide = wide * wide
            for k in range(0, chunk, 128):
                squares[r] = squares[r] + wide[:, k : k + 128]
    mean = jnp.concatenate(squares, axis=0)
    mean = jnp.sum(mean, axis=1, keepdims=True) * (1.0 / width)
    inv_rms = lax.rsqrt(mean + 1e-06)
    for c in range(chunks):
        at = pl.ds(c * chunk, chunk)
        normed_ref[:, at] = (shaped_ref[:, at].astype(F32) * inv_rms).astype(BF16)

    t_at = lax.broadcasted_iota(jnp.int32, (length, 128), 0)
    lane = lax.broadcasted_iota(jnp.int32, (length, 128), 1)
    for r in range(rows):
        move = move_s[r]
        count = lengths_s[r]
        valid = t_at < count
        here = slice(r * length, (r + 1) * length)
        own = jnp.where(valid[:, 0:1], cotangent_v[r].astype(F32), 0.0)
        own_ref[here, :] = jnp.where(move == 0, own, 0.0).astype(BF16)
        marks = jnp.where(lane == 0, inv_rms[here], 0.0)
        marks = jnp.where((lane == 1) & valid & (move == 1), 1.0, marks)
        marks = jnp.where((lane == 2) & valid & (move == -1), 1.0, marks)
        marks = jnp.where((lane == 3) & jnp.logical_not(span[r]), 1.0, marks)
        marks = jnp.where((lane == 4) & valid & (move == 0), 1.0, marks)
        marks_ref[here, :] = jnp.where(lane == 5, jnp.maximum(count, 1).astype(F32), marks)
    for copy in copies[8:]:
        copy.wait()


def forward(
    chunk,
    rows,
    w_ref,
    normed_ref,
    marks_ref,
    wide_ref,
    soft_ref,
    context_ref,
):
    tokens, width = normed_ref.shape
    length = tokens // rows
    head = w_ref.shape[2]
    totals = []
    for i in range(3):
        total = None
        for c in range(width // chunk):
            at = pl.ds(c * chunk, chunk)
            part = dot(normed_ref[:, at], w_ref[i, at, :], ((1,), (0,)))
            total = part if total is None else total + part
        wide_ref[i] = total
        totals.append(total.astype(BF16))
    query, key, value = totals

    marks = marks_ref[...]
    factor = 1.0 / math.sqrt(head)
    q_at = lax.broadcasted_iota(jnp.int32, (tokens, tokens), 0)
    k_at = lax.broadcasted_iota(jnp.int32, (tokens, tokens), 1)
    low = jnp.where(q_at < length, 0, length)
    for r in range(2, rows):
        low = jnp.where(q_at < r * length, low, r * length)
    offset = (k_at - low).astype(F32)
    ok = (offset >= 0.0) & (offset < marks[:, 5:6])
    scores = jnp.where(ok, dot(query, key, ((1,), (1,))) * factor, -jnp.inf)
    exp_scores = jnp.exp(scores - jnp.max(scores, axis=1, keepdims=True))
    soft = exp_scores / jnp.sum(exp_scores, axis=1, keepdims=True)
    soft_ref[...] = soft
    context = dot(soft.astype(BF16), value, ((1,), (0,)))

    def only(lane):
        return jnp.where(marks[:, lane : lane + 1] == 1.0, context, 0.0)

    def one_of(picked):
        return sum(picked[r * length : (r + 1) * length] for r in range(rows)).astype(BF16)

    stays = only(4).astype(BF16)
    for r in range(rows):
        context_ref[r] = stays[r * length : (r + 1) * length]
    context_ref[rows] = one_of(only(1))
    context_ref[rows + 1] = one_of(only(2))


def emit(chunk, gradients, w_ref, shaped_ref, inv_rms, inner, keep, out_ref):
    pieces, rows, per_row, width = out_ref.shape
    length = shaped_ref.shape[0] // rows
    scale = jnp.where(keep, inv_rms, 0.0)
    back = inv_rms * inner
    for c in range(width // chunk):
        at = pl.ds(c * chunk, chunk)
        total = None
        for i in range(3):
            part = dot(gradients[i], w_ref[i, at, :], ((1,), (1,)))
            total = part if total is None else total + part
        part = ((total - shaped_ref[:, at].astype(F32) * back) * scale).astype(BF16)
        for d in range(pieces):
            for r in range(rows):
                low = r * length + d * per_row
                out_ref[d, r, :, at] = part[low : low + per_row]


def backward(
    chunk,
    w_ref,
    shaped_ref,
    marks_ref,
    wide_ref,
    soft_ref,
    own_ref,
    context_ref,
    got_mate_ref,
    got_other_ref,
    out_ref,
    pay_mate_ref,
    pay_other_ref,
):
    rows = out_ref.shape[1]
    width = shaped_ref.shape[1]
    head = w_ref.shape[2]

    even = is_even()
    right, left = context_ref[rows], context_ref[rows + 1]
    pay_mate_ref[...] = jnp.where(even, right, left)
    pay_other_ref[...] = jnp.where(even, left, right)
    from_right = jnp.where(even, got_mate_ref[...], got_other_ref[...]).astype(F32)
    from_left = jnp.where(even, got_other_ref[...], got_mate_ref[...]).astype(F32)
    marks = marks_ref[...]
    inv_rms = marks[:, 0:1]
    grad_out = jnp.where(
        marks[:, 1:2] == 1.0,
        jnp.concatenate([from_right] * rows, axis=0),
        jnp.where(
            marks[:, 2:3] == 1.0,
            jnp.concatenate([from_left] * rows, axis=0),
            own_ref[...].astype(F32),
        ),
    ).astype(BF16)

    factor = 1.0 / math.sqrt(head)
    soft = soft_ref[...]
    query, key, value = (wide_ref[i].astype(BF16) for i in range(3))
    grad_value = dot(soft.astype(BF16), grad_out, ((0,), (0,))).astype(BF16)
    grad_soft = dot(grad_out, value, ((1,), (1,)))
    row_inner = jnp.sum(soft * grad_soft, axis=1, keepdims=True)
    grad_scores = (soft * (grad_soft - row_inner) * factor).astype(BF16)
    grad_query = dot(grad_scores, key, ((1,), (0,))).astype(BF16)
    grad_key = dot(grad_scores, query, ((0,), (0,))).astype(BF16)
    gradients = (grad_query, grad_key, grad_value)
    inner = sum(gradients[i].astype(F32) * wide_ref[i] for i in range(3))
    inner = jnp.sum(inner, axis=1, keepdims=True) * (1.0 / width)
    emit(chunk, gradients, w_ref, shaped_ref, inv_rms, inner, marks[:, 3:4] == 1.0, out_ref)


def assemble(context_ref, got_mate_ref, got_other_ref, out_ref):
    rows = context_ref.shape[0] // 2
    even = is_even()
    got_mate = got_mate_ref[...]
    got_other = got_other_ref[...]
    for r in range(rows):
        out_ref[r] = context_ref[r]
    out_ref[rows] = jnp.where(even, got_other, got_mate)
    out_ref[rows + 1] = jnp.where(even, got_mate, got_other)


def add_heads(heads_ref, out_ref):
    total = heads_ref[0].astype(F32)
    for h in range(1, heads_ref.shape[0]):
        total = total + heads_ref[h].astype(F32)
    out_ref[...] = total.astype(BF16)


def exchange(array, pairs):
    return lax.ppermute(array, "dp", pairs)


def shards(
    inputs,
    denoiser,
    span_mask,
    lengths,
    move_plan,
    mode_table,
    sentinel,
    w_query,
    w_key,
    w_value,
    cotangent,
):
    rows, length, width = inputs.shape
    head = w_query.shape[1]
    tokens = rows * length
    groups = lax.axis_size("dp")
    members = lax.axis_size("mp")
    seg = length // members
    chunk = 512
    vmem = pl.BlockSpec(memory_space=pltpu.VMEM)
    hbm = pl.BlockSpec(memory_space=pltpu.HBM)
    params = pltpu.CompilerParams(vmem_limit_bytes=24 * MIB)
    mates = [(g, g ^ 1) for g in range(groups)]
    others = [(g, (g + 1) % groups if g % 2 else (g - 1) % groups) for g in range(groups)]

    def shape(dims, dtype):
        return jax.ShapeDtypeStruct(dims, dtype)

    slot = shape((length, head), BF16)
    shaped, normed, w_all, marks, own, pay_mate, pay_other = pl.pallas_call(
        lambda *refs: prepare(chunk, *refs),
        out_shape=(
            shape((tokens, width), BF16),
            shape((tokens, width), BF16),
            shape((3, width, head), BF16),
            shape((tokens, 128), F32),
            shape((tokens, head), BF16),
            slot,
            slot,
        ),
        in_specs=[hbm] * 11,
        out_specs=[vmem] * 7,
        scratch_shapes=[
            pltpu.VMEM((rows, length, width), BF16),
            pltpu.VMEM(span_mask.shape, jnp.int32),
            pltpu.VMEM(mode_table.shape, BF16),
            pltpu.VMEM((width,), BF16),
            pltpu.VMEM(cotangent.shape, BF16),
            pltpu.SMEM((rows,), jnp.int32),
            pltpu.SMEM((rows,), jnp.int32),
            pltpu.SMEM((rows,), jnp.int32),
            pltpu.SemaphoreType.DMA((11,)),
        ],
        compiler_params=params,
        name="prepare",
    )(
        *(
            pltpu.with_memory_space_constraint(array, pltpu.HBM)
            for array in (
                inputs,
                denoiser,
                span_mask,
                lengths,
                move_plan,
                mode_table,
                sentinel,
                cotangent,
                w_query,
                w_key,
                w_value,
            )
        )
    )
    cotangent_other = exchange(pay_other, others)
    cotangent_mate = exchange(pay_mate, mates)

    wide, soft, context = pl.pallas_call(
        lambda *refs: forward(chunk, rows, *refs),
        out_shape=(
            shape((3, tokens, head), F32),
            shape((tokens, tokens), F32),
            shape((2 * rows, length, head), BF16),
        ),
        in_specs=[vmem] * 3,
        out_specs=[vmem] * 3,
        compiler_params=params,
        name="forward",
    )(w_all, normed, marks)

    head_part, pay_mate, pay_other = pl.pallas_call(
        lambda *refs: backward(chunk, *refs),
        out_shape=(shape((members, rows, seg, width), BF16), slot, slot),
        in_specs=[vmem] * 9,
        out_specs=[vmem] * 3,
        compiler_params=params,
        name="backward",
    )(
        w_all,
        shaped,
        marks,
        wide,
        soft,
        own,
        context,
        cotangent_mate,
        cotangent_other,
    )
    heads = lax.all_to_all(head_part, "mp", 0, 0)
    got_other = exchange(pay_other, others)
    got_mate = exchange(pay_mate, mates)
    context = pl.pallas_call(
        assemble,
        out_shape=shape(context.shape, BF16),
        in_specs=[vmem] * 3,
        out_specs=vmem,
        name="assemble",
    )(context, got_mate, got_other)
    input_grad = pl.pallas_call(
        add_heads,
        out_shape=shape((rows, seg, width), BF16),
        in_specs=[vmem],
        out_specs=vmem,
        compiler_params=params,
        name="add_heads",
    )(heads)
    return (context, input_grad)


def solution(mesh):
    return jax.shard_map(
        shards,
        mesh=mesh,
        in_specs=(
            P("dp", None, None),
            P("dp"),
            P("dp", None),
            P("dp"),
            P("dp"),
            P(),
            P(),
            P(None, "mp"),
            P(None, "mp"),
            P(None, "mp"),
            P("dp", None, "mp"),
        ),
        out_specs=(P("dp", None, "mp"), P("dp", "mp", None)),
        check_vma=False,
    )
```

```python
import math

import jax
import jax.numpy as jnp
from jax import lax
from jax.experimental import pallas as pl
from jax.experimental.pallas import tpu as pltpu
from jax.sharding import PartitionSpec as P

F32 = jnp.float32
BF16 = jnp.bfloat16
MIB = 1024 * 1024
WINDOW = 3


def column(values):
    size = values.shape[1]
    diagonal = lax.broadcasted_iota(jnp.int32, (size, size), 0) == lax.broadcasted_iota(
        jnp.int32, (size, size), 1
    )
    spread = jnp.where(diagonal, jnp.broadcast_to(values, (size, size)).astype(F32), 0.0)
    return jnp.sum(spread, axis=1, keepdims=True)


def dot(a, b, contract):
    return lax.dot_general(a, b, (contract, ((), ())), preferred_element_type=F32)


def is_even():
    return lax.rem(lax.axis_index("dp"), 2) == 0


def prepare(
    chunk,
    inputs_hbm,
    denoiser_hbm,
    span_hbm,
    lengths_hbm,
    move_hbm,
    mode_hbm,
    sentinel_hbm,
    cotangent_hbm,
    w_query_hbm,
    w_key_hbm,
    w_value_hbm,
    shaped_ref,
    normed_ref,
    w_ref,
    marks_ref,
    own_ref,
    pay_mate_ref,
    pay_other_ref,
    inputs_v,
    span_v,
    mode_v,
    sentinel_v,
    cotangent_v,
    denoiser_s,
    lengths_s,
    move_s,
    sem,
):
    rows, length, width = inputs_v.shape
    tokens = rows * length
    chunks = width // chunk
    copies = [
        pltpu.make_async_copy(source, target, sem.at[i])
        for i, (source, target) in enumerate(
            (
                (inputs_hbm, inputs_v),
                (cotangent_hbm, cotangent_v),
                (mode_hbm, mode_v),
                (sentinel_hbm, sentinel_v),
                (span_hbm, span_v),
                (denoiser_hbm, denoiser_s),
                (lengths_hbm, lengths_s),
                (move_hbm, move_s),
                (w_query_hbm, w_ref.at[0]),
                (w_key_hbm, w_ref.at[1]),
                (w_value_hbm, w_ref.at[2]),
            )
        )
    ]
    for copy in copies:
        copy.start()
    for copy in copies[:8]:
        copy.wait()

    even = is_even()
    to_right, to_left = cotangent_v[rows + 1], cotangent_v[rows]
    pay_mate_ref[...] = jnp.where(even, to_right, to_left)
    pay_other_ref[...] = jnp.where(even, to_left, to_right)

    span = [column(span_v[r : r + 1, :]) == 1.0 for r in range(rows)]
    squares = [jnp.zeros((length, 128), F32) for _ in range(rows)]
    for c in range(chunks):
        at = pl.ds(c * chunk, chunk)
        table = mode_v[:, at].astype(F32)
        sentinel = sentinel_v[at].astype(F32).reshape(1, chunk)
        for r in range(rows):
            kind = denoiser_s[r]
            mode = jnp.where(kind == 0, table[0:1], jnp.where(kind == 1, table[1:2], table[2:3]))
            shaped = jnp.where(span[r], sentinel, inputs_v[r, :, at].astype(F32) + mode)
            shaped = shaped.astype(BF16)
            shaped_ref[r * length : (r + 1) * length, at] = shaped
            wide = shaped.astype(F32)
            wide = wide * wide
            for k in range(0, chunk, 128):
                squares[r] = squares[r] + wide[:, k : k + 128]
    mean = jnp.concatenate(squares, axis=0)
    mean = jnp.sum(mean, axis=1, keepdims=True) * (1.0 / width)
    inv_rms = lax.rsqrt(mean + 1e-06)
    for c in range(chunks):
        at = pl.ds(c * chunk, chunk)
        normed_ref[:, at] = (shaped_ref[:, at].astype(F32) * inv_rms).astype(BF16)

    t_at = lax.broadcasted_iota(jnp.int32, (length, 128), 0)
    lane = lax.broadcasted_iota(jnp.int32, (length, 128), 1)
    for r in range(rows):
        move = move_s[r]
        count = lengths_s[r]
        valid = t_at < count
        here = slice(r * length, (r + 1) * length)
        own = jnp.where(valid[:, 0:1], cotangent_v[r].astype(F32), 0.0)
        own_ref[here, :] = jnp.where(move == 0, own, 0.0).astype(BF16)
        marks = jnp.where(lane == 0, inv_rms[here], 0.0)
        marks = jnp.where((lane == 1) & valid & (move == 1), 1.0, marks)
        marks = jnp.where((lane == 2) & valid & (move == -1), 1.0, marks)
        marks = jnp.where((lane == 3) & jnp.logical_not(span[r]), 1.0, marks)
        marks = jnp.where((lane == 4) & valid & (move == 0), 1.0, marks)
        marks_ref[here, :] = jnp.where(lane == 5, jnp.maximum(count, 1).astype(F32), marks)
    for copy in copies[8:]:
        copy.wait()


def forward(
    chunk,
    rows,
    w_ref,
    normed_ref,
    marks_ref,
    wide_ref,
    soft_ref,
    context_ref,
):
    tokens, width = normed_ref.shape
    length = tokens // rows
    head = w_ref.shape[2]
    totals = []
    for i in range(3):
        total = None
        for c in range(width // chunk):
            at = pl.ds(c * chunk, chunk)
            part = dot(normed_ref[:, at], w_ref[i, at, :], ((1,), (0,)))
            total = part if total is None else total + part
        wide_ref[i] = total
        totals.append(total.astype(BF16))
    query, key, value = totals

    marks = marks_ref[...]
    factor = 1.0 / math.sqrt(head)
    q_at = lax.broadcasted_iota(jnp.int32, (tokens, tokens), 0)
    k_at = lax.broadcasted_iota(jnp.int32, (tokens, tokens), 1)
    low = jnp.where(q_at < length, 0, length)
    for r in range(2, rows):
        low = jnp.where(q_at < r * length, low, r * length)
    offset = (k_at - low).astype(F32)
    ok = (offset >= 0.0) & (offset < marks[:, 5:6])
    scores = jnp.where(ok, dot(query, key, ((1,), (1,))) * factor, -jnp.inf)
    exp_scores = jnp.exp(scores - jnp.max(scores, axis=1, keepdims=True))
    soft = exp_scores / jnp.sum(exp_scores, axis=1, keepdims=True)
    soft_ref[...] = soft
    context = dot(soft.astype(BF16), value, ((1,), (0,)))

    def only(lane):
        return jnp.where(marks[:, lane : lane + 1] == 1.0, context, 0.0)

    def one_of(picked):
        return sum(picked[r * length : (r + 1) * length] for r in range(rows)).astype(BF16)

    stays = only(4).astype(BF16)
    for r in range(rows):
        context_ref[r] = stays[r * length : (r + 1) * length]
    context_ref[rows] = one_of(only(1))
    context_ref[rows + 1] = one_of(only(2))


def order_rows(tokens, rows, members):
    per_row = tokens // rows // members
    piece = rows * per_row
    row_at = lax.broadcasted_iota(jnp.int32, (tokens, tokens), 0)
    from_at = lax.broadcasted_iota(jnp.int32, (tokens, tokens), 1)
    mine = lax.rem(lax.axis_index("mp"), WINDOW)
    want = jnp.full((tokens, tokens), -1, jnp.int32)
    for i in range(tokens // per_row):
        block, left = divmod(i, tokens // WINDOW // per_row)
        j, r = divmod(left, rows)
        member = WINDOW * j + lax.rem(mine + block, WINDOW)
        first = r * (tokens // rows) + member * per_row
        here = (row_at >= i * per_row) & (row_at < (i + 1) * per_row)
        want = jnp.where(here, first + row_at - i * per_row, want)
    return jnp.where(from_at == want, 1.0, 0.0).astype(BF16)


def emit(chunk, rows, gradients, w_ref, shaped_ref, inv_rms, inner, keep, out_refs):
    tokens, width = shaped_ref.shape
    pieces, piece, _ = out_refs[0].shape
    scale = jnp.where(keep, inv_rms, 0.0)
    back = inv_rms * inner
    order = order_rows(tokens, rows, pieces * WINDOW)
    for c in range(width // chunk):
        at = pl.ds(c * chunk, chunk)
        total = None
        for i in range(3):
            part = dot(gradients[i], w_ref[i, at, :], ((1,), (1,)))
            total = part if total is None else total + part
        part = ((total - shaped_ref[:, at].astype(F32) * back) * scale).astype(BF16)
        part = dot(order, part, ((1,), (0,))).astype(BF16)
        for s in range(WINDOW):
            for j in range(pieces):
                low = (s * pieces + j) * piece
                out_refs[s][j, :, at] = part[low : low + piece]


def backward(
    chunk,
    w_ref,
    shaped_ref,
    marks_ref,
    wide_ref,
    soft_ref,
    own_ref,
    got_mate_ref,
    got_other_ref,
    *out_refs,
):
    tokens, width = shaped_ref.shape
    rows = tokens // got_mate_ref.shape[0]
    head = w_ref.shape[2]

    even = is_even()
    from_right = jnp.where(even, got_mate_ref[...], got_other_ref[...]).astype(F32)
    from_left = jnp.where(even, got_other_ref[...], got_mate_ref[...]).astype(F32)
    marks = marks_ref[...]
    inv_rms = marks[:, 0:1]
    grad_out = jnp.where(
        marks[:, 1:2] == 1.0,
        jnp.concatenate([from_right] * rows, axis=0),
        jnp.where(
            marks[:, 2:3] == 1.0,
            jnp.concatenate([from_left] * rows, axis=0),
            own_ref[...].astype(F32),
        ),
    ).astype(BF16)

    factor = 1.0 / math.sqrt(head)
    soft = soft_ref[...]
    query, key, value = (wide_ref[i].astype(BF16) for i in range(3))
    grad_value = dot(soft.astype(BF16), grad_out, ((0,), (0,))).astype(BF16)
    grad_soft = dot(grad_out, value, ((1,), (1,)))
    row_inner = jnp.sum(soft * grad_soft, axis=1, keepdims=True)
    grad_scores = (soft * (grad_soft - row_inner) * factor).astype(BF16)
    grad_query = dot(grad_scores, key, ((1,), (0,))).astype(BF16)
    grad_key = dot(grad_scores, query, ((0,), (0,))).astype(BF16)
    gradients = (grad_query, grad_key, grad_value)
    inner = sum(gradients[i].astype(F32) * wide_ref[i] for i in range(3))
    inner = jnp.sum(inner, axis=1, keepdims=True) * (1.0 / width)
    emit(chunk, rows, gradients, w_ref, shaped_ref, inv_rms, inner, marks[:, 3:4] == 1.0, out_refs)


def combine(
    keep_ref, got_left_ref, got_right_ref, context_ref, got_mate_ref, out_ref, pay_other_ref
):
    del got_mate_ref
    total = keep_ref[...].astype(F32) + got_left_ref[...].astype(F32)
    out_ref[...] = (total + got_right_ref[...].astype(F32)).astype(BF16)
    rows = context_ref.shape[0] // 2
    pay_other_ref[...] = jnp.where(is_even(), context_ref[rows + 1], context_ref[rows])


def address(keep_ref, context_ref, pay_mate_ref):
    del keep_ref
    rows = context_ref.shape[0] // 2
    pay_mate_ref[...] = jnp.where(is_even(), context_ref[rows], context_ref[rows + 1])


def finish(heads_ref, context_ref, got_mate_ref, got_other_ref, context_out_ref, out_ref):
    rows = context_ref.shape[0] // 2
    even = is_even()
    got_mate = got_mate_ref[...]
    got_other = got_other_ref[...]
    for r in range(rows):
        context_out_ref[r] = context_ref[r]
    context_out_ref[rows] = jnp.where(even, got_other, got_mate)
    context_out_ref[rows + 1] = jnp.where(even, got_mate, got_other)
    total = heads_ref[0].astype(F32)
    for h in range(1, heads_ref.shape[0]):
        total = total + heads_ref[h].astype(F32)
    per_row = out_ref.shape[1]
    for r in range(out_ref.shape[0]):
        out_ref[r] = total[r * per_row : (r + 1) * per_row].astype(BF16)


def exchange(array, pairs):
    return lax.ppermute(array, "dp", pairs)


def shards(
    inputs,
    denoiser,
    span_mask,
    lengths,
    move_plan,
    mode_table,
    sentinel,
    w_query,
    w_key,
    w_value,
    cotangent,
):
    rows, length, width = inputs.shape
    head = w_query.shape[1]
    tokens = rows * length
    groups = lax.axis_size("dp")
    members = lax.axis_size("mp")
    seg = length // members
    chunk = 512
    vmem = pl.BlockSpec(memory_space=pltpu.VMEM)
    hbm = pl.BlockSpec(memory_space=pltpu.HBM)
    params = pltpu.CompilerParams(vmem_limit_bytes=24 * MIB)
    mates = [(g, g ^ 1) for g in range(groups)]
    others = [(g, (g + 1) % groups if g % 2 else (g - 1) % groups) for g in range(groups)]

    def shape(dims, dtype):
        return jax.ShapeDtypeStruct(dims, dtype)

    slot = shape((length, head), BF16)
    shaped, normed, w_all, marks, own, pay_mate, pay_other = pl.pallas_call(
        lambda *refs: prepare(chunk, *refs),
        out_shape=(
            shape((tokens, width), BF16),
            shape((tokens, width), BF16),
            shape((3, width, head), BF16),
            shape((tokens, 128), F32),
            shape((tokens, head), BF16),
            slot,
            slot,
        ),
        in_specs=[hbm] * 11,
        out_specs=[vmem] * 7,
        scratch_shapes=[
            pltpu.VMEM((rows, length, width), BF16),
            pltpu.VMEM(span_mask.shape, jnp.int32),
            pltpu.VMEM(mode_table.shape, BF16),
            pltpu.VMEM((width,), BF16),
            pltpu.VMEM(cotangent.shape, BF16),
            pltpu.SMEM((rows,), jnp.int32),
            pltpu.SMEM((rows,), jnp.int32),
            pltpu.SMEM((rows,), jnp.int32),
            pltpu.SemaphoreType.DMA((11,)),
        ],
        compiler_params=params,
        name="prepare",
    )(
        *(
            pltpu.with_memory_space_constraint(array, pltpu.HBM)
            for array in (
                inputs,
                denoiser,
                span_mask,
                lengths,
                move_plan,
                mode_table,
                sentinel,
                cotangent,
                w_query,
                w_key,
                w_value,
            )
        )
    )
    cotangent_other = exchange(pay_other, others)
    cotangent_mate = exchange(pay_mate, mates)

    wide, soft, context = pl.pallas_call(
        lambda *refs: forward(chunk, rows, *refs),
        out_shape=(
            shape((3, tokens, head), F32),
            shape((tokens, tokens), F32),
            shape((2 * rows, length, head), BF16),
        ),
        in_specs=[vmem] * 3,
        out_specs=[vmem] * 3,
        compiler_params=params,
        name="forward",
    )(w_all, normed, marks)

    part = shape((members // WINDOW, rows * seg, width), BF16)
    keep, to_right, to_left = pl.pallas_call(
        lambda *refs: backward(width, *refs),
        out_shape=(part, part, part),
        in_specs=[vmem] * 8,
        out_specs=[vmem] * 3,
        compiler_params=params,
        name="backward",
    )(w_all, shaped, marks, wide, soft, own, cotangent_mate, cotangent_other)
    from_left = lax.ppermute(to_right, "mp", [(m, (m + 1) % members) for m in range(members)])
    from_right = lax.ppermute(to_left, "mp", [(m, (m - 1) % members) for m in range(members)])
    pay_mate = pl.pallas_call(
        address,
        out_shape=slot,
        in_specs=[vmem] * 2,
        out_specs=vmem,
        compiler_params=params,
        name="address",
    )(keep, context)
    got_mate = exchange(pay_mate, mates)
    windows, pay_other = pl.pallas_call(
        combine,
        out_shape=(part, slot),
        in_specs=[vmem] * 5,
        out_specs=[vmem] * 2,
        compiler_params=params,
        name="combine",
    )(keep, from_left, from_right, context, got_mate)
    got_other = exchange(pay_other, others)
    spread = [list(range(c, members, WINDOW)) for c in range(WINDOW)]
    heads = lax.all_to_all(windows, "mp", 0, 0, axis_index_groups=spread)
    context, input_grad = pl.pallas_call(
        finish,
        out_shape=(shape(context.shape, BF16), shape((rows, seg, width), BF16)),
        in_specs=[vmem] * 4,
        out_specs=[vmem] * 2,
        compiler_params=params,
        name="finish",
    )(heads, context, got_mate, got_other)
    return (context, input_grad)


def solution(mesh):
    return jax.shard_map(
        shards,
        mesh=mesh,
        in_specs=(
            P("dp", None, None),
            P("dp"),
            P("dp", None),
            P("dp"),
            P("dp"),
            P(),
            P(),
            P(None, "mp"),
            P(None, "mp"),
            P(None, "mp"),
            P("dp", None, "mp"),
        ),
        out_specs=(P("dp", None, "mp"), P("dp", "mp", None)),
        check_vma=False,
    )
```

```python
import math

import jax
import jax.numpy as jnp
from jax import lax
from jax.experimental import pallas as pl
from jax.experimental.pallas import tpu as pltpu
from jax.sharding import PartitionSpec as P

F32 = jnp.float32
BF16 = jnp.bfloat16
MIB = 1024 * 1024
WINDOW = 3


def column(values):
    size = values.shape[1]
    diagonal = lax.broadcasted_iota(jnp.int32, (size, size), 0) == lax.broadcasted_iota(
        jnp.int32, (size, size), 1
    )
    spread = jnp.where(diagonal, jnp.broadcast_to(values, (size, size)).astype(F32), 0.0)
    return jnp.sum(spread, axis=1, keepdims=True)


def dot(a, b, contract):
    return lax.dot_general(a, b, (contract, ((), ())), preferred_element_type=F32)


def is_even():
    return lax.rem(lax.axis_index("dp"), 2) == 0


def forward(
    chunk,
    inputs_hbm,
    denoiser_hbm,
    span_hbm,
    lengths_hbm,
    move_hbm,
    mode_hbm,
    sentinel_hbm,
    cotangent_hbm,
    w_query_hbm,
    w_key_hbm,
    w_value_hbm,
    shaped_ref,
    w_ref,
    turned_ref,
    marks_ref,
    own_ref,
    wide_ref,
    soft_ref,
    context_ref,
    inputs_v,
    normed_v,
    span_v,
    mode_v,
    sentinel_v,
    cotangent_v,
    denoiser_s,
    lengths_s,
    move_s,
    sem,
):
    rows, length, width = inputs_v.shape
    tokens = rows * length
    chunks = width // chunk
    copies = [
        pltpu.make_async_copy(source, target, sem.at[i])
        for i, (source, target) in enumerate(
            (
                (inputs_hbm, inputs_v),
                (cotangent_hbm.at[pl.ds(0, rows)], cotangent_v),
                (mode_hbm, mode_v),
                (sentinel_hbm, sentinel_v),
                (span_hbm, span_v),
                (denoiser_hbm, denoiser_s),
                (lengths_hbm, lengths_s),
                (move_hbm, move_s),
                (w_query_hbm, w_ref.at[0]),
                (w_key_hbm, w_ref.at[1]),
                (w_value_hbm, w_ref.at[2]),
            )
        )
    ]
    for copy in copies:
        copy.start()
    for copy in copies[:8]:
        copy.wait()

    span = [column(span_v[r : r + 1, :]) == 1.0 for r in range(rows)]
    squares = [jnp.zeros((length, 128), F32) for _ in range(rows)]
    for c in range(chunks):
        at = pl.ds(c * chunk, chunk)
        table = mode_v[:, at].astype(F32)
        sentinel = sentinel_v[at].astype(F32).reshape(1, chunk)
        for r in range(rows):
            kind = denoiser_s[r]
            mode = jnp.where(kind == 0, table[0:1], jnp.where(kind == 1, table[1:2], table[2:3]))
            shaped = jnp.where(span[r], sentinel, inputs_v[r, :, at].astype(F32) + mode)
            shaped = shaped.astype(BF16)
            shaped_ref[r * length : (r + 1) * length, at] = shaped
            wide = shaped.astype(F32)
            wide = wide * wide
            for k in range(0, chunk, 128):
                squares[r] = squares[r] + wide[:, k : k + 128]
    mean = jnp.concatenate(squares, axis=0)
    mean = jnp.sum(mean, axis=1, keepdims=True) * (1.0 / width)
    inv_rms = lax.rsqrt(mean + 1e-06)
    for c in range(chunks):
        at = pl.ds(c * chunk, chunk)
        normed_v[:, at] = (shaped_ref[:, at].astype(F32) * inv_rms).astype(BF16)

    t_at = lax.broadcasted_iota(jnp.int32, (length, 128), 0)
    lane = lax.broadcasted_iota(jnp.int32, (length, 128), 1)
    for r in range(rows):
        move = move_s[r]
        count = lengths_s[r]
        valid = t_at < count
        here = slice(r * length, (r + 1) * length)
        own = jnp.where(valid[:, 0:1], cotangent_v[r].astype(F32), 0.0)
        own_ref[here, :] = jnp.where(move == 0, own, 0.0).astype(BF16)
        marks = jnp.where(lane == 0, inv_rms[here], 0.0)
        marks = jnp.where((lane == 1) & valid & (move == 1), 1.0, marks)
        marks = jnp.where((lane == 2) & valid & (move == -1), 1.0, marks)
        marks = jnp.where((lane == 3) & jnp.logical_not(span[r]), 1.0, marks)
        marks = jnp.where((lane == 4) & valid & (move == 0), 1.0, marks)
        marks_ref[here, :] = jnp.where(lane == 5, jnp.maximum(count, 1).astype(F32), marks)

    marks = marks_ref[...]
    head = w_ref.shape[2]

    def project(i):
        copies[8 + i].wait()
        total = dot(normed_v[...], w_ref[i], ((1,), (0,)))
        wide_ref[i] = total
        if i < turned_ref.shape[0]:
            turned_ref[i] = w_ref[i].T
        return total.astype(BF16)

    query = project(0)
    key = project(1)
    factor = 1.0 / math.sqrt(head)
    q_at = lax.broadcasted_iota(jnp.int32, (tokens, tokens), 0)
    k_at = lax.broadcasted_iota(jnp.int32, (tokens, tokens), 1)
    low = jnp.where(q_at < length, 0, length)
    for r in range(2, rows):
        low = jnp.where(q_at < r * length, low, r * length)
    offset = (k_at - low).astype(F32)
    ok = (offset >= 0.0) & (offset < marks[:, 5:6])
    scores = jnp.where(ok, dot(query, key, ((1,), (1,))) * factor, -jnp.inf)
    exp_scores = jnp.exp(scores - jnp.max(scores, axis=1, keepdims=True))
    soft = exp_scores / jnp.sum(exp_scores, axis=1, keepdims=True)
    soft_ref[...] = soft
    context = dot(soft.astype(BF16), project(2), ((1,), (0,)))

    def only(lane):
        return jnp.where(marks[:, lane : lane + 1] == 1.0, context, 0.0)

    def one_of(picked):
        return sum(picked[r * length : (r + 1) * length] for r in range(rows)).astype(BF16)

    stays = only(4).astype(BF16)
    for r in range(rows):
        context_ref[r] = stays[r * length : (r + 1) * length]
    context_ref[rows] = one_of(only(1))
    context_ref[rows + 1] = one_of(only(2))


def order_rows(tokens, rows, members):
    per_row = tokens // rows // members
    piece = rows * per_row
    row_at = lax.broadcasted_iota(jnp.int32, (tokens, tokens), 0)
    from_at = lax.broadcasted_iota(jnp.int32, (tokens, tokens), 1)
    mine = lax.rem(lax.axis_index("mp"), WINDOW)
    want = jnp.full((tokens, tokens), -1, jnp.int32)
    for i in range(tokens // per_row):
        block, left = divmod(i, tokens // WINDOW // per_row)
        j, r = divmod(left, rows)
        member = WINDOW * j + lax.rem(mine + block, WINDOW)
        first = r * (tokens // rows) + member * per_row
        here = (row_at >= i * per_row) & (row_at < (i + 1) * per_row)
        want = jnp.where(here, first + row_at - i * per_row, want)
    return jnp.where(from_at == want, 1.0, 0.0).astype(BF16)


def emit(chunk, rows, gradients, w_ref, turned_ref, shaped_ref, inv_rms, inner, keep, out_refs):
    tokens, width = shaped_ref.shape
    pieces, piece, _ = out_refs[0].shape
    scale = jnp.where(keep, inv_rms, 0.0)
    back = inv_rms * inner
    order = order_rows(tokens, rows, pieces * WINDOW)
    for c in range(width // chunk):
        at = pl.ds(c * chunk, chunk)
        total = None
        for i in range(3):
            if i < turned_ref.shape[0]:
                part = dot(gradients[i], turned_ref[i, :, at], ((1,), (0,)))
            else:
                part = dot(gradients[i], w_ref[i, at, :], ((1,), (1,)))
            total = part if total is None else total + part
        part = ((total - shaped_ref[:, at].astype(F32) * back) * scale).astype(BF16)
        part = dot(order, part, ((1,), (0,))).astype(BF16)
        for s in range(WINDOW):
            for j in range(pieces):
                low = (s * pieces + j) * piece
                out_refs[s][j, :, at] = part[low : low + piece]


def backward(
    chunk,
    w_ref,
    turned_ref,
    shaped_ref,
    marks_ref,
    wide_ref,
    soft_ref,
    own_ref,
    got_other_ref,
    got_mate_ref,
    *out_refs,
):
    tokens, width = shaped_ref.shape
    rows = tokens // got_mate_ref.shape[1]
    head = w_ref.shape[2]

    even = is_even()
    from_right = jnp.where(even, got_mate_ref[rows], got_other_ref[rows]).astype(F32)
    from_left = jnp.where(even, got_other_ref[rows + 1], got_mate_ref[rows + 1]).astype(F32)
    marks = marks_ref[...]
    inv_rms = marks[:, 0:1]
    grad_out = jnp.where(
        marks[:, 1:2] == 1.0,
        jnp.concatenate([from_right] * rows, axis=0),
        jnp.where(
            marks[:, 2:3] == 1.0,
            jnp.concatenate([from_left] * rows, axis=0),
            own_ref[...].astype(F32),
        ),
    ).astype(BF16)

    factor = 1.0 / math.sqrt(head)
    soft = soft_ref[...]
    query, key, value = (wide_ref[i].astype(BF16) for i in range(3))
    grad_value = dot(soft.astype(BF16), grad_out, ((0,), (0,))).astype(BF16)
    grad_soft = dot(grad_out, value, ((1,), (1,)))
    row_inner = jnp.sum(soft * grad_soft, axis=1, keepdims=True)
    grad_scores = (soft * (grad_soft - row_inner) * factor).astype(BF16)
    grad_query = dot(grad_scores, key, ((1,), (0,))).astype(BF16)
    grad_key = dot(grad_scores, query, ((0,), (0,))).astype(BF16)
    gradients = (grad_query, grad_key, grad_value)
    inner = sum(gradients[i].astype(F32) * wide_ref[i] for i in range(3))
    inner = jnp.sum(inner, axis=1, keepdims=True) * (1.0 / width)
    emit(chunk, rows, gradients, w_ref, turned_ref, shaped_ref, inv_rms, inner, marks[:, 3:4] == 1.0, out_refs)


def combine(
    keep_ref, got_left_ref, got_right_ref, context_ref, got_mate_ref, out_ref, pay_other_ref
):
    del got_mate_ref
    total = keep_ref[...].astype(F32) + got_left_ref[...].astype(F32)
    out_ref[...] = (total + got_right_ref[...].astype(F32)).astype(BF16)
    rows = context_ref.shape[0] // 2
    pay_other_ref[...] = jnp.where(is_even(), context_ref[rows + 1], context_ref[rows])


def address(keep_ref, context_ref, pay_mate_ref):
    del keep_ref
    rows = context_ref.shape[0] // 2
    pay_mate_ref[...] = jnp.where(is_even(), context_ref[rows], context_ref[rows + 1])


def finish(heads_ref, context_ref, got_mate_ref, got_other_ref, context_out_ref, out_ref):
    rows = context_ref.shape[0] // 2
    even = is_even()
    got_mate = got_mate_ref[...]
    got_other = got_other_ref[...]
    for r in range(rows):
        context_out_ref[r] = context_ref[r]
    context_out_ref[rows] = jnp.where(even, got_other, got_mate)
    context_out_ref[rows + 1] = jnp.where(even, got_mate, got_other)
    total = heads_ref[0].astype(F32)
    for h in range(1, heads_ref.shape[0]):
        total = total + heads_ref[h].astype(F32)
    per_row = out_ref.shape[1]
    for r in range(out_ref.shape[0]):
        out_ref[r] = total[r * per_row : (r + 1) * per_row].astype(BF16)


def exchange(array, pairs):
    return lax.ppermute(array, "dp", pairs)


def shards(
    inputs,
    denoiser,
    span_mask,
    lengths,
    move_plan,
    mode_table,
    sentinel,
    w_query,
    w_key,
    w_value,
    cotangent,
):
    rows, length, width = inputs.shape
    head = w_query.shape[1]
    tokens = rows * length
    groups = lax.axis_size("dp")
    members = lax.axis_size("mp")
    seg = length // members
    chunk = 512
    vmem = pl.BlockSpec(memory_space=pltpu.VMEM)
    hbm = pl.BlockSpec(memory_space=pltpu.HBM)
    params = pltpu.CompilerParams(vmem_limit_bytes=24 * MIB)
    mates = [(g, g ^ 1) for g in range(groups)]
    others = [(g, (g + 1) % groups if g % 2 else (g - 1) % groups) for g in range(groups)]

    def shape(dims, dtype):
        return jax.ShapeDtypeStruct(dims, dtype)

    slot = shape((length, head), BF16)
    cotangent_mate = exchange(cotangent, mates)
    cotangent_other = exchange(cotangent, others)
    shaped, w_all, turned, marks, own, wide, soft, context = pl.pallas_call(
        lambda *refs: forward(chunk, *refs),
        out_shape=(
            shape((tokens, width), BF16),
            shape((3, width, head), BF16),
            shape((2, head, width), BF16),
            shape((tokens, 128), F32),
            shape((tokens, head), BF16),
            shape((3, tokens, head), F32),
            shape((tokens, tokens), F32),
            shape((2 * rows, length, head), BF16),
        ),
        in_specs=[hbm] * 11,
        out_specs=[vmem] * 8,
        scratch_shapes=[
            pltpu.VMEM((rows, length, width), BF16),
            pltpu.VMEM((tokens, width), BF16),
            pltpu.VMEM(span_mask.shape, jnp.int32),
            pltpu.VMEM(mode_table.shape, BF16),
            pltpu.VMEM((width,), BF16),
            pltpu.VMEM((rows, length, head), BF16),
            pltpu.SMEM((rows,), jnp.int32),
            pltpu.SMEM((rows,), jnp.int32),
            pltpu.SMEM((rows,), jnp.int32),
            pltpu.SemaphoreType.DMA((11,)),
        ],
        compiler_params=params,
        name="forward",
    )(
        *(
            pltpu.with_memory_space_constraint(array, pltpu.HBM)
            for array in (
                inputs,
                denoiser,
                span_mask,
                lengths,
                move_plan,
                mode_table,
                sentinel,
                cotangent,
                w_query,
                w_key,
                w_value,
            )
        )
    )

    part = shape((members // WINDOW, rows * seg, width), BF16)
    keep, to_right, to_left = pl.pallas_call(
        lambda *refs: backward(width, *refs),
        out_shape=(part, part, part),
        in_specs=[vmem] * 9,
        out_specs=[vmem] * 3,
        compiler_params=params,
        name="backward",
    )(w_all, turned, shaped, marks, wide, soft, own, cotangent_other, cotangent_mate)
    from_left = lax.ppermute(to_right, "mp", [(m, (m + 1) % members) for m in range(members)])
    from_right = lax.ppermute(to_left, "mp", [(m, (m - 1) % members) for m in range(members)])
    pay_mate = pl.pallas_call(
        address,
        out_shape=slot,
        in_specs=[vmem] * 2,
        out_specs=vmem,
        compiler_params=params,
        name="address",
    )(keep, context)
    got_mate = exchange(pay_mate, mates)
    windows, pay_other = pl.pallas_call(
        combine,
        out_shape=(part, slot),
        in_specs=[vmem] * 5,
        out_specs=[vmem] * 2,
        compiler_params=params,
        name="combine",
    )(keep, from_left, from_right, context, got_mate)
    got_other = exchange(pay_other, others)
    spread = [list(range(c, members, WINDOW)) for c in range(WINDOW)]
    heads = lax.all_to_all(windows, "mp", 0, 0, axis_index_groups=spread)
    context, input_grad = pl.pallas_call(
        finish,
        out_shape=(shape(context.shape, BF16), shape((rows, seg, width), BF16)),
        in_specs=[vmem] * 4,
        out_specs=[vmem] * 2,
        compiler_params=params,
        name="finish",
    )(heads, context, got_mate, got_other)
    return (context, input_grad)


def solution(mesh):
    return jax.shard_map(
        shards,
        mesh=mesh,
        in_specs=(
            P("dp", None, None),
            P("dp"),
            P("dp", None),
            P("dp"),
            P("dp"),
            P(),
            P(),
            P(None, "mp"),
            P(None, "mp"),
            P(None, "mp"),
            P("dp", None, "mp"),
        ),
        out_specs=(P("dp", None, "mp"), P("dp", "mp", None)),
        check_vma=False,
    )
```

```python
import math

import jax
import jax.numpy as jnp
from jax import lax
from jax.experimental import pallas as pl
from jax.experimental.pallas import tpu as pltpu
from jax.sharding import PartitionSpec as P

F32 = jnp.float32
BF16 = jnp.bfloat16
MIB = 1024 * 1024
WINDOW = 3


def column(values):
    size = values.shape[1]
    diagonal = lax.broadcasted_iota(jnp.int32, (size, size), 0) == lax.broadcasted_iota(
        jnp.int32, (size, size), 1
    )
    spread = jnp.where(diagonal, jnp.broadcast_to(values, (size, size)).astype(F32), 0.0)
    return jnp.sum(spread, axis=1, keepdims=True)


def dot(a, b, contract):
    return lax.dot_general(a, b, (contract, ((), ())), preferred_element_type=F32)


def is_even():
    return lax.rem(lax.axis_index("dp"), 2) == 0


def forward(
    chunk,
    inputs_hbm,
    denoiser_hbm,
    span_hbm,
    lengths_hbm,
    move_hbm,
    mode_hbm,
    sentinel_hbm,
    cotangent_hbm,
    w_query_hbm,
    w_key_hbm,
    w_value_hbm,
    shaped_ref,
    turned_ref,
    marks_ref,
    own_ref,
    wide_ref,
    soft_ref,
    context_ref,
    inputs_v,
    normed_v,
    w_v,
    span_v,
    mode_v,
    sentinel_v,
    cotangent_v,
    denoiser_s,
    lengths_s,
    move_s,
    sem,
):
    rows, length, width = inputs_v.shape
    tokens = rows * length
    chunks = width // chunk
    copies = [
        pltpu.make_async_copy(source, target, sem.at[i])
        for i, (source, target) in enumerate(
            (
                (inputs_hbm, inputs_v),
                (cotangent_hbm.at[pl.ds(0, rows)], cotangent_v),
                (mode_hbm, mode_v),
                (sentinel_hbm, sentinel_v),
                (span_hbm, span_v),
                (denoiser_hbm, denoiser_s),
                (lengths_hbm, lengths_s),
                (move_hbm, move_s),
                (w_query_hbm, w_v.at[0]),
                (w_key_hbm, w_v.at[1]),
                (w_value_hbm, w_v.at[2]),
            )
        )
    ]
    for copy in copies:
        copy.start()
    for copy in copies[:8]:
        copy.wait()

    span = [column(span_v[r : r + 1, :]) == 1.0 for r in range(rows)]
    squares = [jnp.zeros((length, 128), F32) for _ in range(rows)]
    for c in range(chunks):
        at = pl.ds(c * chunk, chunk)
        table = mode_v[:, at].astype(F32)
        sentinel = sentinel_v[at].astype(F32).reshape(1, chunk)
        for r in range(rows):
            kind = denoiser_s[r]
            mode = jnp.where(kind == 0, table[0:1], jnp.where(kind == 1, table[1:2], table[2:3]))
            shaped = jnp.where(span[r], sentinel, inputs_v[r, :, at].astype(F32) + mode)
            shaped = shaped.astype(BF16)
            shaped_ref[r * length : (r + 1) * length, at] = shaped
            wide = shaped.astype(F32)
            wide = wide * wide
            for k in range(0, chunk, 128):
                squares[r] = squares[r] + wide[:, k : k + 128]
    mean = jnp.concatenate(squares, axis=0)
    mean = jnp.sum(mean, axis=1, keepdims=True) * (1.0 / width)
    inv_rms = lax.rsqrt(mean + 1e-06)
    for c in range(chunks):
        at = pl.ds(c * chunk, chunk)
        normed_v[:, at] = (shaped_ref[:, at].astype(F32) * inv_rms).astype(BF16)

    t_at = lax.broadcasted_iota(jnp.int32, (length, 128), 0)
    lane = lax.broadcasted_iota(jnp.int32, (length, 128), 1)
    for r in range(rows):
        move = move_s[r]
        count = lengths_s[r]
        valid = t_at < count
        here = slice(r * length, (r + 1) * length)
        own = jnp.where(valid[:, 0:1], cotangent_v[r].astype(F32), 0.0)
        own_ref[here, :] = jnp.where(move == 0, own, 0.0).astype(BF16)
        marks = jnp.where(lane == 0, inv_rms[here], 0.0)
        marks = jnp.where((lane == 1) & valid & (move == 1), 1.0, marks)
        marks = jnp.where((lane == 2) & valid & (move == -1), 1.0, marks)
        marks = jnp.where((lane == 3) & jnp.logical_not(span[r]), 1.0, marks)
        marks = jnp.where((lane == 4) & valid & (move == 0), 1.0, marks)
        marks_ref[here, :] = jnp.where(lane == 5, jnp.maximum(count, 1).astype(F32), marks)

    marks = marks_ref[...]
    head = w_v.shape[2]

    def project(i):
        copies[8 + i].wait()
        total = dot(normed_v[...], w_v[i], ((1,), (0,)))
        wide_ref[i] = total
        turned_ref[i] = w_v[i].T
        return total.astype(BF16)

    query = project(0)
    key = project(1)
    factor = 1.0 / math.sqrt(head)
    q_at = lax.broadcasted_iota(jnp.int32, (tokens, tokens), 0)
    k_at = lax.broadcasted_iota(jnp.int32, (tokens, tokens), 1)
    low = jnp.where(q_at < length, 0, length)
    for r in range(2, rows):
        low = jnp.where(q_at < r * length, low, r * length)
    offset = (k_at - low).astype(F32)
    ok = (offset >= 0.0) & (offset < marks[:, 5:6])
    scores = jnp.where(ok, dot(query, key, ((1,), (1,))) * factor, -jnp.inf)
    exp_scores = jnp.exp(scores - jnp.max(scores, axis=1, keepdims=True))
    soft = exp_scores / jnp.sum(exp_scores, axis=1, keepdims=True)
    soft_ref[...] = soft
    context = dot(soft.astype(BF16), project(2), ((1,), (0,)))

    def only(lane):
        return jnp.where(marks[:, lane : lane + 1] == 1.0, context, 0.0)

    def one_of(picked):
        return sum(picked[r * length : (r + 1) * length] for r in range(rows)).astype(BF16)

    stays = only(4).astype(BF16)
    for r in range(rows):
        context_ref[r] = stays[r * length : (r + 1) * length]
    context_ref[rows] = one_of(only(1))
    context_ref[rows + 1] = one_of(only(2))


def order_rows(tokens, rows, members):
    per_row = tokens // rows // members
    piece = rows * per_row
    row_at = lax.broadcasted_iota(jnp.int32, (tokens, tokens), 0)
    from_at = lax.broadcasted_iota(jnp.int32, (tokens, tokens), 1)
    mine = lax.rem(lax.axis_index("mp"), WINDOW)
    want = jnp.full((tokens, tokens), -1, jnp.int32)
    for i in range(tokens // per_row):
        block, left = divmod(i, tokens // WINDOW // per_row)
        j, r = divmod(left, rows)
        member = WINDOW * j + lax.rem(mine + block, WINDOW)
        first = r * (tokens // rows) + member * per_row
        here = (row_at >= i * per_row) & (row_at < (i + 1) * per_row)
        want = jnp.where(here, first + row_at - i * per_row, want)
    return jnp.where(from_at == want, 1.0, 0.0).astype(BF16)


def emit(chunk, rows, gradients, turned_ref, shaped_ref, inv_rms, inner, keep, out_refs):
    tokens, width = shaped_ref.shape
    pieces, piece, _ = out_refs[0].shape
    scale = jnp.where(keep, inv_rms, 0.0)
    back = inv_rms * inner
    order = order_rows(tokens, rows, pieces * WINDOW)
    for c in range(width // chunk):
        at = pl.ds(c * chunk, chunk)
        total = None
        for i in range(3):
            part = dot(gradients[i], turned_ref[i, :, at], ((1,), (0,)))
            total = part if total is None else total + part
        part = ((total - shaped_ref[:, at].astype(F32) * back) * scale).astype(BF16)
        part = dot(order, part, ((1,), (0,)))
        for s in range(WINDOW):
            for j in range(pieces):
                low = (s * pieces + j) * piece
                out_refs[s][j, :, at] = part[low : low + piece].astype(BF16)


def backward(
    chunk,
    turned_ref,
    shaped_ref,
    marks_ref,
    wide_ref,
    soft_ref,
    own_ref,
    got_other_ref,
    got_mate_ref,
    *out_refs,
):
    tokens, width = shaped_ref.shape
    rows = tokens // got_mate_ref.shape[1]
    head = turned_ref.shape[1]

    even = is_even()
    from_right = jnp.where(even, got_mate_ref[rows], got_other_ref[rows]).astype(F32)
    from_left = jnp.where(even, got_other_ref[rows + 1], got_mate_ref[rows + 1]).astype(F32)
    marks = marks_ref[...]
    inv_rms = marks[:, 0:1]
    grad_out = jnp.where(
        marks[:, 1:2] == 1.0,
        jnp.concatenate([from_right] * rows, axis=0),
        jnp.where(
            marks[:, 2:3] == 1.0,
            jnp.concatenate([from_left] * rows, axis=0),
            own_ref[...].astype(F32),
        ),
    ).astype(BF16)

    factor = 1.0 / math.sqrt(head)
    soft = soft_ref[...]
    query, key, value = (wide_ref[i].astype(BF16) for i in range(3))
    grad_value = dot(soft.astype(BF16), grad_out, ((0,), (0,))).astype(BF16)
    grad_soft = dot(grad_out, value, ((1,), (1,)))
    row_inner = jnp.sum(soft * grad_soft, axis=1, keepdims=True)
    grad_scores = (soft * (grad_soft - row_inner) * factor).astype(BF16)
    grad_query = dot(grad_scores, key, ((1,), (0,))).astype(BF16)
    grad_key = dot(grad_scores, query, ((0,), (0,))).astype(BF16)
    gradients = (grad_query, grad_key, grad_value)
    inner = sum(gradients[i].astype(F32) * wide_ref[i] for i in range(3))
    inner = jnp.sum(inner, axis=1, keepdims=True) * (1.0 / width)
    emit(chunk, rows, gradients, turned_ref, shaped_ref, inv_rms, inner, marks[:, 3:4] == 1.0, out_refs)


def combine(
    keep_ref, got_left_ref, got_right_ref, context_ref, got_mate_ref, out_ref, pay_other_ref
):
    del got_mate_ref
    total = keep_ref[...].astype(F32) + got_left_ref[...].astype(F32)
    out_ref[...] = (total + got_right_ref[...].astype(F32)).astype(BF16)
    rows = context_ref.shape[0] // 2
    pay_other_ref[...] = jnp.where(is_even(), context_ref[rows + 1], context_ref[rows])


def address(keep_ref, context_ref, pay_mate_ref):
    del keep_ref
    rows = context_ref.shape[0] // 2
    pay_mate_ref[...] = jnp.where(is_even(), context_ref[rows], context_ref[rows + 1])


def finish(heads_ref, context_ref, got_mate_ref, got_other_ref, context_out_ref, out_ref):
    rows = context_ref.shape[0] // 2
    even = is_even()
    got_mate = got_mate_ref[...]
    got_other = got_other_ref[...]
    for r in range(rows):
        context_out_ref[r] = context_ref[r]
    context_out_ref[rows] = jnp.where(even, got_other, got_mate)
    context_out_ref[rows + 1] = jnp.where(even, got_mate, got_other)
    total = heads_ref[0].astype(F32)
    for h in range(1, heads_ref.shape[0]):
        total = total + heads_ref[h].astype(F32)
    per_row = out_ref.shape[1]
    for r in range(out_ref.shape[0]):
        out_ref[r] = total[r * per_row : (r + 1) * per_row].astype(BF16)


def exchange(array, pairs):
    return lax.ppermute(array, "dp", pairs)


def shards(
    inputs,
    denoiser,
    span_mask,
    lengths,
    move_plan,
    mode_table,
    sentinel,
    w_query,
    w_key,
    w_value,
    cotangent,
):
    rows, length, width = inputs.shape
    head = w_query.shape[1]
    tokens = rows * length
    groups = lax.axis_size("dp")
    members = lax.axis_size("mp")
    seg = length // members
    chunk = 512
    vmem = pl.BlockSpec(memory_space=pltpu.VMEM)
    hbm = pl.BlockSpec(memory_space=pltpu.HBM)
    params = pltpu.CompilerParams(vmem_limit_bytes=24 * MIB)
    mates = [(g, g ^ 1) for g in range(groups)]
    others = [(g, (g + 1) % groups if g % 2 else (g - 1) % groups) for g in range(groups)]

    def shape(dims, dtype):
        return jax.ShapeDtypeStruct(dims, dtype)

    slot = shape((length, head), BF16)
    cotangent_mate = exchange(cotangent, mates)
    cotangent_other = exchange(cotangent, others)
    shaped, turned, marks, own, wide, soft, context = pl.pallas_call(
        lambda *refs: forward(chunk, *refs),
        out_shape=(
            shape((tokens, width), BF16),
            shape((3, head, width), BF16),
            shape((tokens, 128), F32),
            shape((tokens, head), BF16),
            shape((3, tokens, head), F32),
            shape((tokens, tokens), F32),
            shape((2 * rows, length, head), BF16),
        ),
        in_specs=[hbm] * 11,
        out_specs=[vmem] * 7,
        scratch_shapes=[
            pltpu.VMEM((rows, length, width), BF16),
            pltpu.VMEM((tokens, width), BF16),
            pltpu.VMEM((3, width, head), BF16),
            pltpu.VMEM(span_mask.shape, jnp.int32),
            pltpu.VMEM(mode_table.shape, BF16),
            pltpu.VMEM((width,), BF16),
            pltpu.VMEM((rows, length, head), BF16),
            pltpu.SMEM((rows,), jnp.int32),
            pltpu.SMEM((rows,), jnp.int32),
            pltpu.SMEM((rows,), jnp.int32),
            pltpu.SemaphoreType.DMA((11,)),
        ],
        compiler_params=params,
        name="forward",
    )(
        *(
            pltpu.with_memory_space_constraint(array, pltpu.HBM)
            for array in (
                inputs,
                denoiser,
                span_mask,
                lengths,
                move_plan,
                mode_table,
                sentinel,
                cotangent,
                w_query,
                w_key,
                w_value,
            )
        )
    )

    part = shape((members // WINDOW, rows * seg, width), BF16)
    keep, to_right, to_left = pl.pallas_call(
        lambda *refs: backward(width, *refs),
        out_shape=(part, part, part),
        in_specs=[vmem] * 8,
        out_specs=[vmem] * 3,
        compiler_params=params,
        name="backward",
    )(turned, shaped, marks, wide, soft, own, cotangent_other, cotangent_mate)
    from_left = lax.ppermute(to_right, "mp", [(m, (m + 1) % members) for m in range(members)])
    from_right = lax.ppermute(to_left, "mp", [(m, (m - 1) % members) for m in range(members)])
    pay_mate = pl.pallas_call(
        address,
        out_shape=slot,
        in_specs=[vmem] * 2,
        out_specs=vmem,
        compiler_params=params,
        name="address",
    )(keep, context)
    got_mate = exchange(pay_mate, mates)
    windows, pay_other = pl.pallas_call(
        combine,
        out_shape=(part, slot),
        in_specs=[vmem] * 5,
        out_specs=[vmem] * 2,
        compiler_params=params,
        name="combine",
    )(keep, from_left, from_right, context, got_mate)
    got_other = exchange(pay_other, others)
    spread = [list(range(c, members, WINDOW)) for c in range(WINDOW)]
    heads = lax.all_to_all(windows, "mp", 0, 0, axis_index_groups=spread)
    context, input_grad = pl.pallas_call(
        finish,
        out_shape=(shape(context.shape, BF16), shape((rows, seg, width), BF16)),
        in_specs=[vmem] * 4,
        out_specs=[vmem] * 2,
        compiler_params=params,
        name="finish",
    )(heads, context, got_mate, got_other)
    return (context, input_grad)


def solution(mesh):
    return jax.shard_map(
        shards,
        mesh=mesh,
        in_specs=(
            P("dp", None, None),
            P("dp"),
            P("dp", None),
            P("dp"),
            P("dp"),
            P(),
            P(),
            P(None, "mp"),
            P(None, "mp"),
            P(None, "mp"),
            P("dp", None, "mp"),
        ),
        out_specs=(P("dp", None, "mp"), P("dp", "mp", None)),
        check_vma=False,
    )
```

```python
import math

import jax
import jax.numpy as jnp
from jax import lax
from jax.experimental import pallas as pl
from jax.experimental.pallas import tpu as pltpu
from jax.sharding import PartitionSpec as P

F32 = jnp.float32
BF16 = jnp.bfloat16
MIB = 1024 * 1024
WINDOW = 3


def column(values):
    size = values.shape[1]
    diagonal = lax.broadcasted_iota(jnp.int32, (size, size), 0) == lax.broadcasted_iota(
        jnp.int32, (size, size), 1
    )
    spread = jnp.where(diagonal, jnp.broadcast_to(values, (size, size)).astype(F32), 0.0)
    return jnp.sum(spread, axis=1, keepdims=True)


def dot(a, b, contract):
    return lax.dot_general(a, b, (contract, ((), ())), preferred_element_type=F32)


def is_even():
    return lax.rem(lax.axis_index("dp"), 2) == 0


def forward(
    chunk,
    members,
    inputs_hbm,
    denoiser_hbm,
    span_hbm,
    lengths_hbm,
    move_hbm,
    mode_hbm,
    sentinel_hbm,
    cotangent_hbm,
    w_query_hbm,
    w_key_hbm,
    w_value_hbm,
    ordered_ref,
    turned_ref,
    marks_ref,
    own_ref,
    wide_ref,
    soft_ref,
    context_ref,
    inputs_v,
    shaped_v,
    normed_v,
    w_v,
    span_v,
    mode_v,
    sentinel_v,
    cotangent_v,
    denoiser_s,
    lengths_s,
    move_s,
    sem,
):
    rows, length, width = inputs_v.shape
    tokens = rows * length
    chunks = width // chunk
    copies = [
        pltpu.make_async_copy(source, target, sem.at[i])
        for i, (source, target) in enumerate(
            (
                (inputs_hbm, inputs_v),
                (cotangent_hbm.at[pl.ds(0, rows)], cotangent_v),
                (mode_hbm, mode_v),
                (sentinel_hbm, sentinel_v),
                (span_hbm, span_v),
                (denoiser_hbm, denoiser_s),
                (lengths_hbm, lengths_s),
                (move_hbm, move_s),
                (w_query_hbm, w_v.at[0]),
                (w_key_hbm, w_v.at[1]),
                (w_value_hbm, w_v.at[2]),
            )
        )
    ]
    for copy in copies:
        copy.start()
    for copy in copies[:8]:
        copy.wait()

    span = [column(span_v[r : r + 1, :]) == 1.0 for r in range(rows)]
    squares = [jnp.zeros((length, 128), F32) for _ in range(rows)]
    for c in range(chunks):
        at = pl.ds(c * chunk, chunk)
        table = mode_v[:, at].astype(F32)
        sentinel = sentinel_v[at].astype(F32).reshape(1, chunk)
        for r in range(rows):
            kind = denoiser_s[r]
            mode = jnp.where(kind == 0, table[0:1], jnp.where(kind == 1, table[1:2], table[2:3]))
            shaped = jnp.where(span[r], sentinel, inputs_v[r, :, at].astype(F32) + mode)
            shaped = shaped.astype(BF16)
            shaped_v[r * length : (r + 1) * length, at] = shaped
            wide = shaped.astype(F32)
            wide = wide * wide
            for k in range(0, chunk, 128):
                squares[r] = squares[r] + wide[:, k : k + 128]
    mean = jnp.concatenate(squares, axis=0)
    mean = jnp.sum(mean, axis=1, keepdims=True) * (1.0 / width)
    inv_rms = lax.rsqrt(mean + 1e-06)
    for c in range(chunks):
        at = pl.ds(c * chunk, chunk)
        normed_v[:, at] = (shaped_v[:, at].astype(F32) * inv_rms).astype(BF16)

    t_at = lax.broadcasted_iota(jnp.int32, (length, 128), 0)
    lane = lax.broadcasted_iota(jnp.int32, (length, 128), 1)
    for r in range(rows):
        move = move_s[r]
        count = lengths_s[r]
        valid = t_at < count
        here = slice(r * length, (r + 1) * length)
        own = jnp.where(valid[:, 0:1], cotangent_v[r].astype(F32), 0.0)
        own_ref[here, :] = jnp.where(move == 0, own, 0.0).astype(BF16)
        marks = jnp.where(lane == 0, inv_rms[here], 0.0)
        marks = jnp.where((lane == 1) & valid & (move == 1), 1.0, marks)
        marks = jnp.where((lane == 2) & valid & (move == -1), 1.0, marks)
        marks = jnp.where((lane == 3) & jnp.logical_not(span[r]), 1.0, marks)
        marks = jnp.where((lane == 4) & valid & (move == 0), 1.0, marks)
        marks_ref[here, :] = jnp.where(lane == 5, jnp.maximum(count, 1).astype(F32), marks)

    order = order_rows(tokens, rows, members)
    ordered_ref[...] = dot(order, shaped_v[...], ((1,), (0,))).astype(BF16)
    marks = marks_ref[...]
    head = w_v.shape[2]

    def project(i):
        copies[8 + i].wait()
        total = dot(normed_v[...], w_v[i], ((1,), (0,)))
        wide_ref[i] = total
        turned_ref[i] = w_v[i].T
        return total.astype(BF16)

    query = project(0)
    key = project(1)
    factor = 1.0 / math.sqrt(head)
    q_at = lax.broadcasted_iota(jnp.int32, (tokens, tokens), 0)
    k_at = lax.broadcasted_iota(jnp.int32, (tokens, tokens), 1)
    low = jnp.where(q_at < length, 0, length)
    for r in range(2, rows):
        low = jnp.where(q_at < r * length, low, r * length)
    offset = (k_at - low).astype(F32)
    ok = (offset >= 0.0) & (offset < marks[:, 5:6])
    scores = jnp.where(ok, dot(query, key, ((1,), (1,))) * factor, -jnp.inf)
    exp_scores = jnp.exp(scores - jnp.max(scores, axis=1, keepdims=True))
    soft = exp_scores / jnp.sum(exp_scores, axis=1, keepdims=True)
    soft_ref[...] = soft
    context = dot(soft.astype(BF16), project(2), ((1,), (0,)))

    def only(lane):
        return jnp.where(marks[:, lane : lane + 1] == 1.0, context, 0.0)

    def one_of(picked):
        return sum(picked[r * length : (r + 1) * length] for r in range(rows)).astype(BF16)

    stays = only(4).astype(BF16)
    for r in range(rows):
        context_ref[r] = stays[r * length : (r + 1) * length]
    context_ref[rows] = one_of(only(1))
    context_ref[rows + 1] = one_of(only(2))


def order_rows(tokens, rows, members):
    per_row = tokens // rows // members
    piece = rows * per_row
    row_at = lax.broadcasted_iota(jnp.int32, (tokens, tokens), 0)
    from_at = lax.broadcasted_iota(jnp.int32, (tokens, tokens), 1)
    member_at = lax.axis_index("mp")
    mine = lax.rem(member_at, WINDOW)
    step = jnp.where(lax.rem(member_at, 2) == 0, 1, WINDOW - 1)
    want = jnp.full((tokens, tokens), -1, jnp.int32)
    for i in range(tokens // per_row):
        block, left = divmod(i, tokens // WINDOW // per_row)
        j, r = divmod(left, rows)
        member = WINDOW * j + lax.rem(mine + block * step, WINDOW)
        first = r * (tokens // rows) + member * per_row
        here = (row_at >= i * per_row) & (row_at < (i + 1) * per_row)
        want = jnp.where(here, first + row_at - i * per_row, want)
    return jnp.where(from_at == want, 1.0, 0.0).astype(BF16)


def emit(rows, gradients, turned_ref, ordered_ref, inv_rms, inner, keep, out_refs):
    tokens = ordered_ref.shape[0]
    pieces, piece, _ = out_refs[0].shape
    order = order_rows(tokens, rows, pieces * WINDOW)
    lane = lax.broadcasted_iota(jnp.int32, (tokens, 128), 1)
    scale = jnp.where(keep, inv_rms, 0.0)
    columns = jnp.where(lane == 0, scale, jnp.where(lane == 1, inv_rms * inner, 0.0))
    columns = lax.dot_general(
        order.astype(F32),
        columns,
        (((1,), (0,)), ((), ())),
        precision=lax.Precision.HIGHEST,
        preferred_element_type=F32,
    )
    total = None
    for i in range(3):
        gradient = dot(order, gradients[i], ((1,), (0,))).astype(BF16)
        part = dot(gradient, turned_ref[i], ((1,), (0,)))
        total = part if total is None else total + part
    part = (total - ordered_ref[...].astype(F32) * columns[:, 1:2]) * columns[:, 0:1]
    for s in range(WINDOW):
        for j in range(pieces):
            low = (s * pieces + j) * piece
            out_refs[s][j] = part[low : low + piece].astype(BF16)


def backward(
    turned_ref,
    ordered_ref,
    marks_ref,
    wide_ref,
    soft_ref,
    own_ref,
    got_other_ref,
    got_mate_ref,
    *out_refs,
):
    tokens, width = ordered_ref.shape
    rows = tokens // got_mate_ref.shape[1]
    head = turned_ref.shape[1]

    even = is_even()
    from_right = jnp.where(even, got_mate_ref[rows], got_other_ref[rows]).astype(F32)
    from_left = jnp.where(even, got_other_ref[rows + 1], got_mate_ref[rows + 1]).astype(F32)
    marks = marks_ref[...]
    inv_rms = marks[:, 0:1]
    grad_out = jnp.where(
        marks[:, 1:2] == 1.0,
        jnp.concatenate([from_right] * rows, axis=0),
        jnp.where(
            marks[:, 2:3] == 1.0,
            jnp.concatenate([from_left] * rows, axis=0),
            own_ref[...].astype(F32),
        ),
    ).astype(BF16)

    factor = 1.0 / math.sqrt(head)
    soft = soft_ref[...]
    query, key, value = (wide_ref[i].astype(BF16) for i in range(3))
    grad_value = dot(soft.astype(BF16), grad_out, ((0,), (0,))).astype(BF16)
    grad_soft = dot(grad_out, value, ((1,), (1,)))
    row_inner = jnp.sum(soft * grad_soft, axis=1, keepdims=True)
    grad_scores = (soft * (grad_soft - row_inner) * factor).astype(BF16)
    grad_query = dot(grad_scores, key, ((1,), (0,))).astype(BF16)
    grad_key = dot(grad_scores, query, ((0,), (0,))).astype(BF16)
    gradients = (grad_query, grad_key, grad_value)
    inner = sum(gradients[i].astype(F32) * wide_ref[i] for i in range(3))
    inner = jnp.sum(inner, axis=1, keepdims=True) * (1.0 / width)
    emit(rows, gradients, turned_ref, ordered_ref, inv_rms, inner, marks[:, 3:4] == 1.0, out_refs)


def combine(
    keep_ref, got_first_ref, got_second_ref, context_ref, got_mate_ref, out_ref, pay_other_ref
):
    del got_mate_ref
    total = keep_ref[...].astype(F32) + got_first_ref[...].astype(F32)
    out_ref[...] = (total + got_second_ref[...].astype(F32)).astype(BF16)
    rows = context_ref.shape[0] // 2
    pay_other_ref[...] = jnp.where(is_even(), context_ref[rows + 1], context_ref[rows])


def address(keep_ref, context_ref, pay_mate_ref):
    del keep_ref
    rows = context_ref.shape[0] // 2
    pay_mate_ref[...] = jnp.where(is_even(), context_ref[rows], context_ref[rows + 1])


def finish(heads_ref, context_ref, got_mate_ref, got_other_ref, context_out_ref, out_ref):
    rows = context_ref.shape[0] // 2
    even = is_even()
    got_mate = got_mate_ref[...]
    got_other = got_other_ref[...]
    for r in range(rows):
        context_out_ref[r] = context_ref[r]
    context_out_ref[rows] = jnp.where(even, got_other, got_mate)
    context_out_ref[rows + 1] = jnp.where(even, got_mate, got_other)
    total = heads_ref[0].astype(F32)
    for h in range(1, heads_ref.shape[0]):
        total = total + heads_ref[h].astype(F32)
    per_row = out_ref.shape[1]
    for r in range(out_ref.shape[0]):
        out_ref[r] = total[r * per_row : (r + 1) * per_row].astype(BF16)


def ring_pairs(size):
    return [(i, (i + 1) % size if i % 2 else (i - 1) % size) for i in range(size)]


def exchange(array, pairs):
    return lax.ppermute(array, "dp", pairs)


def shards(
    inputs,
    denoiser,
    span_mask,
    lengths,
    move_plan,
    mode_table,
    sentinel,
    w_query,
    w_key,
    w_value,
    cotangent,
):
    rows, length, width = inputs.shape
    head = w_query.shape[1]
    tokens = rows * length
    groups = lax.axis_size("dp")
    members = lax.axis_size("mp")
    seg = length // members
    chunk = 512
    vmem = pl.BlockSpec(memory_space=pltpu.VMEM)
    hbm = pl.BlockSpec(memory_space=pltpu.HBM)
    params = pltpu.CompilerParams(vmem_limit_bytes=24 * MIB)
    mates = [(g, g ^ 1) for g in range(groups)]
    others = ring_pairs(groups)

    def shape(dims, dtype):
        return jax.ShapeDtypeStruct(dims, dtype)

    slot = shape((length, head), BF16)
    cotangent_mate = exchange(cotangent, mates)
    cotangent_other = exchange(cotangent, others)
    shaped, turned, marks, own, wide, soft, context = pl.pallas_call(
        lambda *refs: forward(chunk, members, *refs),
        out_shape=(
            shape((tokens, width), BF16),
            shape((3, head, width), BF16),
            shape((tokens, 128), F32),
            shape((tokens, head), BF16),
            shape((3, tokens, head), F32),
            shape((tokens, tokens), F32),
            shape((2 * rows, length, head), BF16),
        ),
        in_specs=[hbm] * 11,
        out_specs=[vmem] * 7,
        scratch_shapes=[
            pltpu.VMEM((rows, length, width), BF16),
            pltpu.VMEM((tokens, width), BF16),
            pltpu.VMEM((tokens, width), BF16),
            pltpu.VMEM((3, width, head), BF16),
            pltpu.VMEM(span_mask.shape, jnp.int32),
            pltpu.VMEM(mode_table.shape, BF16),
            pltpu.VMEM((width,), BF16),
            pltpu.VMEM((rows, length, head), BF16),
            pltpu.SMEM((rows,), jnp.int32),
            pltpu.SMEM((rows,), jnp.int32),
            pltpu.SMEM((rows,), jnp.int32),
            pltpu.SemaphoreType.DMA((11,)),
        ],
        compiler_params=params,
        name="forward",
    )(
        *(
            pltpu.with_memory_space_constraint(array, pltpu.HBM)
            for array in (
                inputs,
                denoiser,
                span_mask,
                lengths,
                move_plan,
                mode_table,
                sentinel,
                cotangent,
                w_query,
                w_key,
                w_value,
            )
        )
    )

    part = shape((members // WINDOW, rows * seg, width), BF16)
    keep, to_first, to_second = pl.pallas_call(
        backward,
        out_shape=(part, part, part),
        in_specs=[vmem] * 8,
        out_specs=[vmem] * 3,
        compiler_params=params,
        name="backward",
    )(turned, shaped, marks, wide, soft, own, cotangent_other, cotangent_mate)
    from_first = lax.ppermute(to_first, "mp", [(m, m ^ 1) for m in range(members)])
    from_second = lax.ppermute(to_second, "mp", ring_pairs(members))
    pay_mate = pl.pallas_call(
        address,
        out_shape=slot,
        in_specs=[vmem] * 2,
        out_specs=vmem,
        compiler_params=params,
        name="address",
    )(keep, context)
    got_mate = exchange(pay_mate, mates)
    windows, pay_other = pl.pallas_call(
        combine,
        out_shape=(part, slot),
        in_specs=[vmem] * 5,
        out_specs=[vmem] * 2,
        compiler_params=params,
        name="combine",
    )(keep, from_first, from_second, context, got_mate)
    got_other = exchange(pay_other, others)
    spread = [list(range(c, members, WINDOW)) for c in range(WINDOW)]
    heads = lax.all_to_all(windows, "mp", 0, 0, axis_index_groups=spread)
    context, input_grad = pl.pallas_call(
        finish,
        out_shape=(shape(context.shape, BF16), shape((rows, seg, width), BF16)),
        in_specs=[vmem] * 4,
        out_specs=[vmem] * 2,
        compiler_params=params,
        name="finish",
    )(heads, context, got_mate, got_other)
    return (context, input_grad)


def solution(mesh):
    return jax.shard_map(
        shards,
        mesh=mesh,
        in_specs=(
            P("dp", None, None),
            P("dp"),
            P("dp", None),
            P("dp"),
            P("dp"),
            P(),
            P(),
            P(None, "mp"),
            P(None, "mp"),
            P(None, "mp"),
            P("dp", None, "mp"),
        ),
        out_specs=(P("dp", None, "mp"), P("dp", "mp", None)),
        check_vma=False,
    )
```
